512 devices in a mesh: blk: 16 (over x, y_lo, core), dp: 32 (over y_hi, z).
Axes of the slice: x: 4, y: 4 (y_hi: 2, y_lo: 2; y = y_hi * 2 + y_lo), z: 16, core: 2. Of those that a mesh axis runs over, the one named last changes fastest.
Arguments:
- users: bfloat16 [32, 4096, 512], P('dp', 'blk'), may hold values from -32 to 32
- items: bfloat16 [32, 4096, 512], P('dp', 'blk'), may hold values from -24 to 24
- weights: float32 [32, 4096], P('dp', 'blk'), may hold values from 0.5 to 18
- positives: int32 [32, 4096], P('dp', 'blk'), may hold values from 0 to 4095, each once within a row
- log_scale: float32 [1], replicated, may hold values from 0 to 1.1
Outputs:
- grad_users: bfloat16 [32, 4096, 512], P('dp', 'blk')
- grad_items: bfloat16 [32, 4096, 512], P('dp', 'blk')
- scale_grad: float32 [1], replicated
The draws below stay inside these ranges and needn't reach their ends.
Inputs may be any that keep to these rules, and one draw needn't show every extreme that they name: For each group g, positives[g] is a permutation of 0 to 4095.
All inputs are finite; a program needn't handle non-finite values.
Results may differ from the reference program's by a relative error of at most 0.0049.
Values may be sent and summed in bfloat16 or wider, within the bound.
A program may use at most 64 MiB of HBM per device.

```python
import math
import jax
import jax.numpy as jnp
from jax import lax

D = 512
GROUP = 4096
GROUPS = 32


def shared_dirs(key):
    dir_key = jax.random.fold_in(key, 0)
    directions = jnp.clip(jax.random.normal(dir_key, (GROUPS, GROUP, D), jnp.float32), -4.0, 4.0)
    return directions


def row_scales(key, low, high):
    return jnp.exp(jax.random.uniform(key, (GROUPS, GROUP, 1), jnp.float32, math.log(low), math.log(high)))


def draw_users(key, part):
    key = jax.random.fold_in(key, 3)
    dir_key, scale_key = jax.random.split(key)
    own_dirs = jnp.clip(jax.random.normal(dir_key, (GROUPS, GROUP, D), jnp.float32), -4.0, 4.0)
    return (own_dirs * row_scales(scale_key, 0.25, 2.5)).astype(jnp.bfloat16)


def draw_items(key, part):
    item_dirs = shared_dirs(key)
    key = jax.random.fold_in(key, 7)
    return (item_dirs * row_scales(key, 0.25, 2.5)).astype(jnp.bfloat16)


def draw_weights(key, part):
    key = jax.random.fold_in(key, 11)
    rise = jnp.arange(GROUPS * GROUP, dtype=jnp.float32).reshape((GROUPS, GROUP)) / (GROUPS * GROUP - 1)
    base = jnp.exp(jax.random.uniform(key, (GROUPS, GROUP), jnp.float32, math.log(0.5), math.log(2.0)))
    return base * (1.0 + 2.0 * rise)


def setup_inputs(seed: int = 0) -> dict:
    keys = jax.random.split(jax.random.key(seed), 6)
    users = draw_users(jax.random.fold_in(keys[5], 71), 0)
    items = draw_items(jax.random.fold_in(keys[5], 71), 0)
    weights = draw_weights(jax.random.fold_in(keys[5], 71), 0)
    positives = jax.vmap(lambda own: jax.random.permutation(own, GROUP))(jax.random.split(keys[3], GROUPS)).reshape((GROUPS, GROUP)).astype(jnp.int32)
    log_scale = jnp.clip(jax.random.uniform(keys[4], (1,), jnp.float32, 0.0, 1.1), 0.0, 1.1)
    return dict(users=users, items=items, weights=weights, positives=positives, log_scale=log_scale)


def group_grads(group_data, logit_scale, norm):
    group_users, group_items, group_weights, group_targets = group_data
    scores = logit_scale * jnp.dot(group_users, group_items.T, preferred_element_type=jnp.float32)
    columns = jnp.arange(GROUP, dtype=jnp.int32)
    hits = (group_targets[:, None] == columns[None, :]).astype(jnp.float32)
    row_lse = jax.nn.logsumexp(scores, axis=1)
    column_lse = jax.nn.logsumexp(scores, axis=0)
    column_weight = lax.optimization_barrier(jnp.sum(group_weights[:, None] * hits, axis=0))
    score_grad = group_weights[:, None] * (jnp.exp(scores - row_lse[:, None]) - hits) + column_weight[None, :] * (jnp.exp(scores - column_lse[None, :]) - hits)
    rounded = score_grad.astype(jnp.bfloat16)
    user_grad = jnp.dot(rounded, group_items, preferred_element_type=jnp.float32)
    item_grad = jnp.dot(rounded.T, group_users, preferred_element_type=jnp.float32)
    user_out = (norm * logit_scale * user_grad).astype(jnp.bfloat16)
    item_out = (norm * logit_scale * item_grad).astype(jnp.bfloat16)
    return (user_out, item_out, jnp.sum(score_grad * scores))

def reference(users, items, weights, positives, log_scale):
    logit_scale = jnp.exp(log_scale[0]) / math.sqrt(D)
    total_weight = jnp.sum(weights)
    norm = GROUPS * GROUP / total_weight
    grad_users, grad_items, scale_parts = lax.map(lambda group_data: group_grads(group_data, logit_scale, norm), (users, items, weights, positives))
    scale_grad = (jnp.sum(scale_parts) / total_weight).reshape((1,))
    return (grad_users, grad_items, scale_grad)
```

```python
import functools
import math

import jax
import jax.numpy as jnp
from jax import lax
from jax.experimental import pallas as pl
from jax.experimental.pallas import tpu as pltpu
from jax.sharding import PartitionSpec as P

MESH = pl.DeviceIdType.MESH
F32 = jnp.float32
BF16 = jnp.bfloat16
LOW = -3.0e38
CHUNK = 32

(
    U_RIGHT_0, U_LEFT_1, U_RIGHT_1, U_LEFT_0, U_RELAY_RIGHT, U_RELAY_LEFT,
    I_CORE, I_Y_0, I_Y_1, I_PASS_0, I_PASS_1,
    WP_1, WP_2, WP_3, CW_1, CW_2, CW_3, RS_1, RS_2, RS_3, CS_1, CS_2, CS_3,
    GU_FAR_RIGHT, GU_FAR_LEFT, GU_RIGHT_0, GU_RIGHT_1, GU_LEFT_0, GU_LEFT_1,
    GI_CORE_0, GI_CORE_1, GI_Y,
    TRANSFERS,
) = range(33)


def dot_nt(a, b):
    return lax.dot_general(a, b, (((1,), (1,)), ((), ())), preferred_element_type=F32)


def dot_tn(a, b):
    return lax.dot_general(a, b, (((0,), (0,)), ((), ())), preferred_element_type=F32)


def fold_rows(block, op):
    total = block[0:8]
    for r in range(8, block.shape[0], 8):
        total = op(total, block[r : r + 8])
    return total


def kernel(
    nx, nyc, n_dp, n_blk,
    users, items, weights, positives, log_scale,
    gu_out, gi_out, scale_out,
    u_all, i_all, wp, t_all, g_all, wcol, pcol, acol, row_m, row_s,
    rowst, colst, cwst, brow,
    far, far_right, far_left, to_left, to_right, from_left, from_right,
    own_gu, own_gi, other_gi, core_0, core_1, got_core_0, got_core_1, to_y, from_y,
    red_dp, red_blk,
    local_sem, send, recv, dp_send, dp_recv, blk_send, blk_recv,
):
    n = users.shape[0]
    width = users.shape[1]
    half = n // 2
    cols = nyc * n
    me = lax.axis_index("blk")
    my_dp = lax.axis_index("dp")
    x = me // nyc
    yc = me % nyc
    core = yc % 2
    y = yc // 2

    def at_x(d):
        return {"blk": ((x + d) % nx) * nyc + yc, "dp": my_dp}

    def at_yc(d):
        c = 1 - core if d % 2 else core
        w = 1 - y if d // 2 else y
        return {"blk": x * nyc + w * 2 + c, "dp": my_dp}

    right, left = at_x(1), at_x(nx - 1)

    def remote(src, dst, number, device):
        return pltpu.make_async_remote_copy(
            src_ref=src, dst_ref=dst, send_sem=send.at[number], recv_sem=recv.at[number],
            device_id=device, device_id_type=MESH,
        )

    own_users = pltpu.make_async_copy(users, u_all.at[pl.ds(0, n)], local_sem.at[0])
    own_items = pltpu.make_async_copy(items, i_all.at[pl.ds(0, n)], local_sem.at[1])
    own_users.start()
    own_items.start()

    barrier = pltpu.get_barrier_semaphore()

    def greet_blk(d, carry):
        pl.semaphore_signal(
            barrier, inc=1, device_id={"blk": (me + d) % n_blk, "dp": my_dp}, device_id_type=MESH
        )
        return carry

    def greet_dp(d, carry):
        pl.semaphore_signal(
            barrier, inc=1, device_id={"blk": me, "dp": (my_dp + d) % n_dp}, device_id_type=MESH
        )
        return carry

    lax.fori_loop(1, n_blk, greet_blk, 0)
    lax.fori_loop(1, n_dp, greet_dp, 0)
    wp[0] = jnp.zeros((8, n), F32)
    wp[0, 0:1, :] = weights[...]
    wp[0, 1:2, :] = positives[...].astype(F32)
    own_users.wait()
    own_items.wait()
    pl.semaphore_wait(barrier, n_blk + n_dp - 2)

    def u_rows(slot, h):
        return u_all.at[pl.ds(slot * n + h * half, half)]

    def i_rows(slot, h):
        return i_all.at[pl.ds(slot * n + h * half, half)]

    started = []

    def start(copy):
        copy.start()
        started.append(copy)
        return copy

    wp_copies = [start(remote(wp.at[0], wp.at[d], WP_1 + d - 1, at_x(d))) for d in (1, 2, 3)]
    u_r0 = start(remote(u_rows(0, 0), u_rows(1, 0), U_RIGHT_0, right))
    u_l1 = start(remote(u_rows(0, 1), u_rows(3, 1), U_LEFT_1, left))
    i_core = start(remote(i_all.at[pl.ds(0, n)], i_all.at[pl.ds(n, n)], I_CORE, at_yc(1)))
    i_y0 = start(remote(i_rows(0, 0), i_rows(2, 0), I_Y_0, at_yc(2)))
    u_r1 = start(remote(u_rows(0, 1), u_rows(1, 1), U_RIGHT_1, right))
    u_l0 = start(remote(u_rows(0, 0), u_rows(3, 0), U_LEFT_0, left))
    i_y1 = start(remote(i_rows(0, 1), i_rows(2, 1), I_Y_1, at_yc(2)))

    k = jnp.exp(jnp.full((1, 2 * n), log_scale[0], F32)) * (1.0 / (math.sqrt(width) * math.log(2.0)))

    def scores(slot, h):
        block = dot_nt(u_all[slot * n : (slot + 1) * n, :], i_all[h * 2 * n : (h + 1) * 2 * n, :])
        t_all[slot * n : (slot + 1) * n, h * 2 * n : (h + 1) * 2 * n] = block * k

    lane = lax.broadcasted_iota(jnp.int32, (1, 128), 1)

    def column_ids(c):
        block, part = c // (n // 128), c % (n // 128)
        owner = at_yc(block)["blk"]
        return (owner * n + part * 128 + lane).astype(F32)

    chunks = cols // 128
    ids = [column_ids(c) for c in range(chunks)]

    for c in wp_copies:
        c.wait_recv()
    for slot in range(nx):
        wcol[slot * n : (slot + 1) * n, :] = jnp.broadcast_to(wp[slot, 0:1, :], (128, n)).T
        pcol[slot * n : (slot + 1) * n, :] = jnp.broadcast_to(wp[slot, 1:2, :], (128, n)).T

    def weigh(i, total):
        rows = pl.ds(pl.multiple_of(i * CHUNK, CHUNK), CHUNK)
        w = wcol[rows, :]
        p = pcol[rows, :]
        return tuple(
            total[c] + fold_rows(jnp.where(p == ids[c], w, 0.0), jnp.add) for c in range(chunks)
        )

    total = lax.fori_loop(
        0, nx * n // CHUNK, weigh, tuple(jnp.zeros((8, 128), F32) for _ in range(chunks))
    )
    cwst[0] = jnp.zeros((8, n), F32)
    per = n // 128
    for c in range(chunks):
        cwst[0, c // per : c // per + 1, (c % per) * 128 : (c % per + 1) * 128] = jnp.sum(
            total[c], axis=0, keepdims=True
        )
    cw_copies = [start(remote(cwst.at[0], cwst.at[d], CW_1 + d - 1, at_yc(d))) for d in (1, 2, 3)]

    i_core.wait_recv()
    scores(0, 0)
    u_r0.wait_recv()
    relay_r = start(remote(u_rows(1, 0), u_rows(2, 0), U_RELAY_RIGHT, right))
    u_l1.wait_recv()
    relay_l = start(remote(u_rows(3, 1), u_rows(2, 1), U_RELAY_LEFT, left))
    i_y0.wait_recv()
    i_p0 = start(remote(i_rows(2, 0), i_rows(3, 0), I_PASS_0, at_yc(1)))
    u_r1.wait_recv()
    i_y1.wait_recv()
    i_p1 = start(remote(i_rows(2, 1), i_rows(3, 1), I_PASS_1, at_yc(1)))
    scores(1, 0)
    u_l0.wait_recv()
    scores(3, 0)
    i_p0.wait_recv()
    i_p1.wait_recv()

    def statistics(slot):
        def maxima(i, best):
            rows = pl.ds(pl.multiple_of(slot * n + i * CHUNK, CHUNK), CHUNK)
            top = None
            out = []
            for c in range(chunks):
                t = t_all[rows, c * 128 : (c + 1) * 128]
                top = t if top is None else jnp.maximum(top, t)
                out.append(jnp.maximum(best[c], fold_rows(t, jnp.maximum)))
            here = pl.ds(pl.multiple_of(i * CHUNK, CHUNK), CHUNK)
            row_m[here, :] = jnp.broadcast_to(jnp.max(top, axis=1, keepdims=True), (CHUNK, 128))
            return tuple(out)

        best = lax.fori_loop(
            0, n // CHUNK, maxima, tuple(jnp.full((8, 128), LOW, F32) for _ in range(chunks))
        )
        best = [jnp.max(b, axis=0, keepdims=True) for b in best]

        def sums(i, total):
            rows = pl.ds(pl.multiple_of(slot * n + i * CHUNK, CHUNK), CHUNK)
            here = pl.ds(pl.multiple_of(i * CHUNK, CHUNK), CHUNK)
            m = row_m[here, :]
            line = None
            out = []
            for c in range(chunks):
                t = t_all[rows, c * 128 : (c + 1) * 128]
                e = jnp.exp2(t - m)
                line = e if line is None else line + e
                out.append(total[c] + fold_rows(jnp.exp2(t - best[c]), jnp.add))
            row_s[here, :] = jnp.broadcast_to(jnp.sum(line, axis=1, keepdims=True), (CHUNK, 128))
            return tuple(out)

        total = lax.fori_loop(
            0, n // CHUNK, sums, tuple(jnp.zeros((8, 128), F32) for _ in range(chunks))
        )
        total = [jnp.sum(b, axis=0, keepdims=True) for b in total]
        first = lax.broadcasted_iota(jnp.int32, (n, 128), 1) == 0
        packed = jnp.where(first, row_m[...], row_s[...]).T
        rowst[0, slot : slot + 1, :] = packed[0:1, :]
        rowst[0, nx + slot : nx + slot + 1, :] = packed[1:2, :]
        return best, total

    parts = {}
    for slot in (0, 1, 3):
        scores(slot, 1)
        parts[slot] = statistics(slot)
    relay_r.wait_recv()
    relay_l.wait_recv()
    scores(2, 0)
    scores(2, 1)
    parts[2] = statistics(2)

    for c in range(chunks):
        m = functools.reduce(jnp.maximum, [parts[s][0][c] for s in range(nx)])
        l = sum(parts[s][1][c] * jnp.exp2(parts[s][0][c] - m) for s in range(nx))
        b, q = c // per, (c % per) * 128
        colst[0, b : b + 1, q : q + 128] = m
        colst[0, nyc + b : nyc + b + 1, q : q + 128] = l

    rs_copies = [start(remote(rowst.at[0], rowst.at[d], RS_1 + d - 1, at_x(d))) for d in (1, 2, 3)]
    cs_copies = [start(remote(colst.at[0], colst.at[d], CS_1 + d - 1, at_yc(d))) for d in (1, 2, 3)]
    for c in cw_copies + cs_copies:
        c.wait_recv()
    for b in range(nyc):
        ms = [colst[d, b ^ d : (b ^ d) + 1, :] for d in range(nyc)]
        ls = [colst[d, nyc + (b ^ d) : nyc + (b ^ d) + 1, :] for d in range(nyc)]
        w = sum(cwst[d, b ^ d : (b ^ d) + 1, :] for d in range(nyc))
        m = functools.reduce(jnp.maximum, ms)
        l = sum(li * jnp.exp2(mi - m) for mi, li in zip(ms, ls))
        brow[0:1, b * n : (b + 1) * n] = m + jnp.log2(l / w)
    for c in rs_copies:
        c.wait_recv()
    for r in range(nx):
        at = [(r - d) % nx for d in range(nx)]
        ms = [rowst[d, at[d] : at[d] + 1, :] for d in range(nx)]
        ls = [rowst[d, nx + at[d] : nx + at[d] + 1, :] for d in range(nx)]
        m = functools.reduce(jnp.maximum, ms)
        l = sum(li * jnp.exp2(mi - m) for mi, li in zip(ms, ls))
        a = m + jnp.log2(l / wp[r, 0:1, :])
        acol[r * n : (r + 1) * n, :] = jnp.broadcast_to(a, (128, n)).T

    b_rows = [brow[0:1, c * 128 : (c + 1) * 128] for c in range(chunks)]

    def gradients(slot, part):
        def step(i, part):
            rows = pl.ds(pl.multiple_of(slot * n + i * CHUNK, CHUNK), CHUNK)
            a = acol[rows, :]
            w2 = 2.0 * wcol[rows, :]
            p = pcol[rows, :]
            for c in range(chunks):
                t = t_all[rows, c * 128 : (c + 1) * 128]
                g = jnp.exp2(t - a) + jnp.exp2(t - b_rows[c])
                g = g - jnp.where(p == ids[c], w2, 0.0)
                part = part + fold_rows(g * t, jnp.add)
                g_all[rows, c * 128 : (c + 1) * 128] = g.astype(BF16)
            return part

        return lax.fori_loop(0, n // CHUNK, step, part)

    def user_part(slot):
        return jnp.dot(
            g_all[slot * n : (slot + 1) * n, :], i_all[...], preferred_element_type=F32
        )

    def item_part(slot):
        return dot_tn(g_all[:, slot * n : (slot + 1) * n], u_all[...])

    part = gradients(2, jnp.zeros((8, 128), F32))
    far[...] = user_part(2).astype(BF16)
    gu_fr = start(remote(far.at[pl.ds(0, half)], far_right, GU_FAR_RIGHT, right))
    gu_fl = start(remote(far.at[pl.ds(half, half)], far_left, GU_FAR_LEFT, left))
    part = gradients(1, part)
    own_gu[...] = user_part(1)
    to_left[0:half, :] = own_gu[0:half, :].astype(BF16)
    gu_l0 = start(remote(to_left.at[pl.ds(0, half)], from_right.at[pl.ds(0, half)], GU_LEFT_0, left))
    part = gradients(3, part)
    own_gi[...] = user_part(3)
    to_right[half:n, :] = own_gi[half:n, :].astype(BF16)
    gu_r1 = start(
        remote(to_right.at[pl.ds(half, half)], from_left.at[pl.ds(half, half)], GU_RIGHT_1, right)
    )
    part = gradients(0, part)

    red_dp[0] = jnp.zeros((8, 128), F32)
    red_dp[0, 0:1, :] = jnp.broadcast_to(jnp.sum(part, keepdims=True) * math.log(2.0), (1, 128))
    red_dp[0, 1:2, :] = jnp.broadcast_to(jnp.sum(wp[0, 0:1, :], keepdims=True), (1, 128))

    def dp_copy(d):
        return pltpu.make_async_remote_copy(
            src_ref=red_dp.at[0], dst_ref=red_dp.at[d], send_sem=dp_send.at[d], recv_sem=dp_recv.at[d],
            device_id={"blk": me, "dp": (my_dp + d) % n_dp}, device_id_type=MESH,
        )

    def blk_copy(d):
        return pltpu.make_async_remote_copy(
            src_ref=red_blk.at[0], dst_ref=red_blk.at[d], send_sem=blk_send.at[d], recv_sem=blk_recv.at[d],
            device_id={"blk": (me + d) % n_blk, "dp": my_dp}, device_id_type=MESH,
        )

    def each(first, last, copy, action):
        def step(d, carry):
            action(copy(d))
            return carry

        lax.fori_loop(first, last, step, 0)

    each(1, n_dp, dp_copy, lambda c: c.start())

    core_0[...] = item_part(1).astype(BF16)
    gi_c0 = start(remote(core_0, got_core_0, GI_CORE_0, at_yc(1)))
    core_1[...] = item_part(3).astype(BF16)
    gi_c1 = start(remote(core_1, got_core_1, GI_CORE_1, at_yc(1)))

    gu_fr.wait_recv()
    to_right[0:half, :] = (own_gi[0:half, :] + far_right[...].astype(F32)).astype(BF16)
    gu_r0 = start(
        remote(to_right.at[pl.ds(0, half)], from_left.at[pl.ds(0, half)], GU_RIGHT_0, right)
    )
    gu_fl.wait_recv()
    to_left[half:n, :] = (own_gu[half:n, :] + far_left[...].astype(F32)).astype(BF16)
    gu_l1 = start(
        remote(to_left.at[pl.ds(half, half)], from_right.at[pl.ds(half, half)], GU_LEFT_1, left)
    )
    other_gi[...] = item_part(2)
    gi_c1.wait_recv()
    to_y[...] = (other_gi[...] + got_core_1[...].astype(F32)).astype(BF16)
    gi_y = start(remote(to_y, from_y, GI_Y, at_yc(2)))

    each(1, n_dp, dp_copy, lambda c: c.wait_recv())
    red_blk[0] = jnp.sum(red_dp[...], axis=0)
    each(1, n_blk, blk_copy, lambda c: c.start())

    own_gu[...] = user_part(0)
    own_gi[...] = item_part(0)
    gi_c0.wait_recv()
    own_gi[...] = own_gi[...] + got_core_0[...].astype(F32)

    each(1, n_blk, blk_copy, lambda c: c.wait_recv())
    sums = jnp.sum(red_blk[...], axis=0)
    weight = sums[1:2, :]
    scale_out[0] = (sums[0:1, :] / weight)[0, 0]
    rows_total = float(n * n_blk * n_dp)
    factor = (rows_total / weight) * (k[:, 0:128] * math.log(2.0))
    factor = jnp.concatenate([factor] * (width // 128), axis=1)

    gu_l0.wait_recv()
    gu_r1.wait_recv()
    gu_r0.wait_recv()
    gu_l1.wait_recv()
    gu_out[...] = (
        factor * (own_gu[...] + from_left[...].astype(F32) + from_right[...].astype(F32))
    ).astype(BF16)
    gi_y.wait_recv()
    gi_out[...] = (factor * (own_gi[...] + from_y[...].astype(F32))).astype(BF16)

    for c in started:
        c.wait_send()
    each(1, n_dp, dp_copy, lambda c: c.wait_send())
    each(1, n_blk, blk_copy, lambda c: c.wait_send())


def body(users, items, weights, positives, log_scale):
    users, items = users[0], items[0]
    n, width = users.shape
    n_blk, n_dp = lax.axis_size("blk"), lax.axis_size("dp")
    nyc = 4
    nx = n_blk // nyc
    any_space = pl.BlockSpec(memory_space=pl.ANY)
    vmem = pl.BlockSpec(memory_space=pltpu.VMEM)
    smem = pl.BlockSpec(memory_space=pltpu.SMEM)
    V = pltpu.VMEM
    rows, cols = nx * n, nyc * n
    half = n // 2
    gu, gi, scale = pl.pallas_call(
        functools.partial(kernel, nx, nyc, n_dp, n_blk),
        out_shape=(
            jax.ShapeDtypeStruct((n, width), BF16),
            jax.ShapeDtypeStruct((n, width), BF16),
            jax.ShapeDtypeStruct((1,), F32),
        ),
        in_specs=[any_space, any_space, vmem, vmem, smem],
        out_specs=(vmem, vmem, smem),
        scratch_shapes=[
            V((rows, width), BF16),
            V((cols, width), BF16),
            V((nx, 8, n), F32),
            V((rows, cols), F32),
            V((rows, cols), BF16),
            V((rows, 128), F32),
            V((rows, 128), F32),
            V((rows, 128), F32),
            V((n, 128), F32),
            V((n, 128), F32),
            V((nx, 8, n), F32),
            V((nyc, 8, n), F32),
            V((nyc, 8, n), F32),
            V((8, cols), F32),
            V((n, width), BF16),
            V((half, width), BF16),
            V((half, width), BF16),
            V((n, width), BF16),
            V((n, width), BF16),
            V((n, width), BF16),
            V((n, width), BF16),
            V((n, width), F32),
            V((n, width), F32),
            V((n, width), F32),
            V((n, width), BF16),
            V((n, width), BF16),
            V((n, width), BF16),
            V((n, width), BF16),
            V((n, width), BF16),
            V((n, width), BF16),
            V((n_dp, 8, 128), F32),
            V((n_blk, 8, 128), F32),
            pltpu.SemaphoreType.DMA((2,)),
            pltpu.SemaphoreType.DMA((TRANSFERS,)),
            pltpu.SemaphoreType.DMA((TRANSFERS,)),
            pltpu.SemaphoreType.DMA((n_dp,)),
            pltpu.SemaphoreType.DMA((n_dp,)),
            pltpu.SemaphoreType.DMA((n_blk,)),
            pltpu.SemaphoreType.DMA((n_blk,)),
        ],
        compiler_params=pltpu.CompilerParams(
            collective_id=0, has_side_effects=True, vmem_limit_bytes=48 * 1024 * 1024
        ),
        cost_estimate=pl.CostEstimate(
            flops=6 * rows * cols * width, bytes_accessed=4 * n * width * 2,
            transcendentals=4 * rows * cols,
        ),
        name="loss_gradients",
    )(users, items, weights, positives, log_scale)
    return gu[None], gi[None], scale


def solution(mesh):
    placed = (P("dp", "blk", None), P("dp", "blk", None), P("dp", "blk"), P("dp", "blk"), P())
    return jax.shard_map(
        body,
        mesh=mesh,
        in_specs=placed,
        out_specs=(P("dp", "blk", None), P("dp", "blk", None), P()),
        check_vma=False,
    )
```

```python
import functools
import math

import jax
import jax.numpy as jnp
from jax import lax
from jax.experimental import pallas as pl
from jax.experimental.pallas import tpu as pltpu
from jax.sharding import PartitionSpec as P

MESH = pl.DeviceIdType.MESH
F32 = jnp.float32
BF16 = jnp.bfloat16
LOW = -3.0e38
CHUNK = 32

(
    U_RIGHT_0, U_LEFT_1, U_RIGHT_1, U_LEFT_0, U_RELAY_RIGHT, U_RELAY_LEFT,
    I_CORE, I_Y_0, I_Y_1, I_PASS_0, I_PASS_1,
    WP_RIGHT, WP_LEFT, WP_RELAY, RS_1, RS_2, RS_3, CS_1, CS_2, CS_3,
    GU_FAR_RIGHT, GU_FAR_LEFT, GU_RIGHT_0, GU_RIGHT_1, GU_LEFT_0, GU_LEFT_1,
    GI_CORE_0, GI_CORE_1, GI_Y,
    TRANSFERS,
) = range(30)


def dot_nt(a, b):
    return lax.dot_general(a, b, (((1,), (1,)), ((), ())), preferred_element_type=F32)


def dot_tn(a, b):
    return lax.dot_general(a, b, (((0,), (0,)), ((), ())), preferred_element_type=F32)


def fold_rows(block, op):
    total = block[0:8]
    for r in range(8, block.shape[0], 8):
        total = op(total, block[r : r + 8])
    return total


def kernel(
    nx, nyc, n_dp, n_blk,
    users, items, weights, positives, log_scale,
    gu_out, gi_out, scale_out,
    u_all, i_all, w_in, p_in, wp, t_all, g_all, wcol, pcol, acol, row_m, lines,
    rowst, colst, brow,
    far, far_right, far_left, to_left, to_right, from_left, from_right,
    own_gu, own_gi, other_gi, core_0, core_1, got_core_0, got_core_1, to_y, from_y,
    red_dp, red_blk,
    local_sem, send, recv, dp_send, dp_recv, blk_send, blk_recv, hello,
):
    n = users.shape[0]
    width = users.shape[1]
    half = n // 2
    cols = nyc * n
    chunks = cols // 128
    per = n // 128
    steps = n // CHUNK
    me = lax.axis_index("blk")
    my_dp = lax.axis_index("dp")
    x = me // nyc
    yc = me % nyc
    core = yc % 2
    y = yc // 2
    depth = n_dp // 2
    rank = (my_dp % depth) * 2 + my_dp // depth

    def at_x(d):
        return {"blk": ((x + d) % nx) * nyc + yc, "dp": my_dp}

    def at_yc(d):
        c = 1 - core if d % 2 else core
        w = 1 - y if d // 2 else y
        return {"blk": x * nyc + w * 2 + c, "dp": my_dp}

    def at_rank(r):
        return {"blk": me, "dp": (r % 2) * depth + r // 2}

    right, left = at_x(1), at_x(nx - 1)

    def remote(src, dst, number, device):
        return pltpu.make_async_remote_copy(
            src_ref=src, dst_ref=dst, send_sem=send.at[number], recv_sem=recv.at[number],
            device_id=device, device_id_type=MESH,
        )

    def loop(first, last, action):
        def step(d, carry):
            action(d)
            return carry

        lax.fori_loop(first, last, step, 0)

    def greet(semaphore, device):
        pl.semaphore_signal(semaphore, inc=1, device_id=device, device_id_type=MESH)

    barrier = pltpu.get_barrier_semaphore()
    for device in (right, left, at_yc(1), at_yc(2)):
        greet(barrier, device)
    locals_ = [
        pltpu.make_async_copy(src, dst, local_sem.at[i])
        for i, (src, dst) in enumerate(
            [
                (users, u_all.at[pl.ds(0, n)]),
                (items, i_all.at[pl.ds(0, n)]),
                (weights, w_in),
                (positives, p_in),
            ]
        )
    ]
    for c in locals_:
        c.start()
    loop(rank + 1, n_dp, lambda r: greet(barrier, at_rank(r)))
    for c in locals_:
        c.wait()
    wp[0] = jnp.zeros((8, n), F32)
    wp[0, 0:1, :] = w_in[...]
    wp[0, 1:2, :] = p_in[...].astype(F32)
    pl.semaphore_wait(barrier, 4 + rank)

    def u_rows(slot, h):
        return u_all.at[pl.ds(slot * n + h * half, half)]

    def i_rows(slot, h):
        return i_all.at[pl.ds(slot * n + h * half, half)]

    started = []

    def start(copy):
        copy.start()
        started.append(copy)
        return copy

    wp_r = start(remote(wp.at[0], wp.at[1], WP_RIGHT, right))
    wp_l = start(remote(wp.at[0], wp.at[3], WP_LEFT, left))
    u_r0 = start(remote(u_rows(0, 0), u_rows(1, 0), U_RIGHT_0, right))
    u_l1 = start(remote(u_rows(0, 1), u_rows(3, 1), U_LEFT_1, left))
    i_y0 = start(remote(i_rows(0, 0), i_rows(2, 0), I_Y_0, at_yc(2)))
    i_core = start(remote(i_all.at[pl.ds(0, n)], i_all.at[pl.ds(n, n)], I_CORE, at_yc(1)))
    u_r1 = start(remote(u_rows(0, 1), u_rows(1, 1), U_RIGHT_1, right))
    u_l0 = start(remote(u_rows(0, 0), u_rows(3, 0), U_LEFT_0, left))
    i_y1 = start(remote(i_rows(0, 1), i_rows(2, 1), I_Y_1, at_yc(2)))
    loop(0, rank, lambda r: greet(hello, at_rank(r)))

    k = jnp.exp(jnp.full((1, 2 * n), log_scale[0], F32)) * (1.0 / (math.sqrt(width) * math.log(2.0)))

    def scores(slot, h):
        block = dot_nt(u_all[slot * n : (slot + 1) * n, :], i_all[h * 2 * n : (h + 1) * 2 * n, :])
        t_all[slot * n : (slot + 1) * n, h * 2 * n : (h + 1) * 2 * n] = block * k

    lane = lax.broadcasted_iota(jnp.int32, (1, 128), 1)

    def column_ids(c):
        block, part = c // per, c % per
        owner = at_yc(block)["blk"]
        return (owner * n + part * 128 + lane).astype(F32)

    ids = [column_ids(c) for c in range(chunks)]

    def spread(slot):
        wcol[slot * n : (slot + 1) * n, :] = jnp.broadcast_to(wp[slot, 0:1, :], (128, n)).T
        pcol[slot * n : (slot + 1) * n, :] = jnp.broadcast_to(wp[slot, 1:2, :], (128, n)).T

    def statistics(slot):
        def maxima(i, best):
            rows = pl.ds(pl.multiple_of(slot * n + i * CHUNK, CHUNK), CHUNK)
            top = None
            out = []
            for c in range(chunks):
                t = t_all[rows, c * 128 : (c + 1) * 128]
                top = t if top is None else jnp.maximum(top, t)
                out.append(jnp.maximum(best[c], fold_rows(t, jnp.maximum)))
            here = pl.ds(pl.multiple_of(i * CHUNK, CHUNK), CHUNK)
            row_m[here, :] = jnp.broadcast_to(jnp.max(top, axis=1, keepdims=True), (CHUNK, 128))
            return tuple(out)

        best = lax.fori_loop(
            0, steps, maxima, tuple(jnp.full((8, 128), LOW, F32) for _ in range(chunks)), unroll=True
        )
        best = [jnp.max(b, axis=0, keepdims=True) for b in best]

        def sums(i, total):
            rows = pl.ds(pl.multiple_of(slot * n + i * CHUNK, CHUNK), CHUNK)
            here = pl.ds(pl.multiple_of(i * CHUNK, CHUNK), CHUNK)
            m = row_m[here, :]
            p = pcol[rows, :]
            w = wcol[rows, :]
            out = []
            line = None
            for c in range(chunks):
                t = t_all[rows, c * 128 : (c + 1) * 128]
                d = t - m
                e = jnp.exp2(d)
                cd = t - best[c]
                ce = jnp.exp2(cd)
                at = p == ids[c]
                hit = jnp.where(at, t, 0.0)
                new = (e, e * d, hit)
                line = new if line is None else tuple(a + b for a, b in zip(line, new))
                for q, v in enumerate((ce, ce * cd, hit, jnp.where(at, w, 0.0))):
                    out.append(total[4 * c + q] + fold_rows(v, jnp.add))
            for q in range(3):
                lines[q, here, :] = line[q]
            return tuple(out)

        total = lax.fori_loop(
            0, steps, sums, tuple(jnp.zeros((8, 128), F32) for _ in range(4 * chunks)), unroll=True
        )
        total = [jnp.sum(b, axis=0, keepdims=True) for b in total]
        rowst[0, slot : slot + 1, :] = row_m[...].T[0:1, :]
        for q in range(3):
            at = (q + 1) * nx + slot
            rowst[0, at : at + 1, :] = jnp.sum(lines[q].T, axis=0, keepdims=True)
        return best, total

    parts = {}
    spread(0)
    i_core.wait_recv()
    scores(0, 0)
    wp_r.wait_recv()
    wp_relay = start(remote(wp.at[1], wp.at[2], WP_RELAY, right))
    spread(1)
    wp_l.wait_recv()
    spread(3)
    u_r0.wait_recv()
    relay_r = start(remote(u_rows(1, 0), u_rows(2, 0), U_RELAY_RIGHT, right))
    u_l1.wait_recv()
    relay_l = start(remote(u_rows(3, 1), u_rows(2, 1), U_RELAY_LEFT, left))
    i_y0.wait_recv()
    i_p0 = start(remote(i_rows(2, 0), i_rows(3, 0), I_PASS_0, at_yc(1)))
    wp_relay.wait_recv()
    spread(2)
    u_r1.wait_recv()
    scores(1, 0)
    u_l0.wait_recv()
    scores(3, 0)
    i_y1.wait_recv()
    i_p1 = start(remote(i_rows(2, 1), i_rows(3, 1), I_PASS_1, at_yc(1)))
    i_p0.wait_recv()
    i_p1.wait_recv()
    for slot in (0, 1, 3):
        scores(slot, 1)
        parts[slot] = statistics(slot)
    relay_r.wait_recv()
    relay_l.wait_recv()
    scores(2, 0)
    scores(2, 1)
    parts[2] = statistics(2)

    rs_copies = [start(remote(rowst.at[0], rowst.at[d], RS_1 + d - 1, at_x(d))) for d in (2, 1, 3)]
    colst[0] = jnp.zeros((24, n), F32)
    for c in range(chunks):
        b, q = c // per, (c % per) * 128
        ms = [parts[s][0][c] for s in range(nx)]
        m = functools.reduce(jnp.maximum, ms)
        l = e = 0.0
        for s in range(nx):
            scale = jnp.exp2(ms[s] - m)
            part_l = parts[s][1][4 * c]
            l = l + scale * part_l
            e = e + scale * (parts[s][1][4 * c + 1] + (ms[s] - m) * part_l)
        hit = sum(parts[s][1][4 * c + 2] for s in range(nx))
        cw = sum(parts[s][1][4 * c + 3] for s in range(nx))
        for i, v in enumerate((m, l, e, hit, cw)):
            colst[0, i * nyc + b : i * nyc + b + 1, q : q + 128] = v
    cs_copies = [start(remote(colst.at[0], colst.at[d], CS_1 + d - 1, at_yc(d))) for d in (3, 2, 1)]

    def combine(source, at, count):
        def rows(i):
            return [source[d, i * count + at[d] : i * count + at[d] + 1, :] for d in range(count)]

        ms, ls, es, hits = rows(0), rows(1), rows(2), rows(3)
        m = functools.reduce(jnp.maximum, ms)
        scales = [jnp.exp2(mi - m) for mi in ms]
        l = sum(li * si for li, si in zip(ls, scales))

        def share():
            e = sum(si * (ei + (mi - m) * li) for mi, li, ei, si in zip(ms, ls, es, scales))
            return e / l - (sum(hits) - m)

        return m, l, share

    for c in cs_copies:
        c.wait_recv()
    part = 0.0
    for b in range(nyc):
        at = [b ^ d for d in range(nyc)]
        m, l, share = combine(colst, at, nyc)
        w = sum(colst[d, 4 * nyc + at[d] : 4 * nyc + at[d] + 1, :] for d in range(nyc))
        brow[0:1, b * n : (b + 1) * n] = m + jnp.log2(l / w)
        if b == 0:
            part = part + w * share()
    for c in rs_copies:
        c.wait_recv()
    for r in (0, 2, 1, 3):
        m, l, share = combine(rowst, [(r - d) % nx for d in range(nx)], nx)
        w = wp[r, 0:1, :]
        if r == 0:
            part = part + w * share()
            red_dp[rank] = jnp.zeros((8, 128), F32)
            red_dp[rank, 0:1, :] = jnp.broadcast_to(
                jnp.sum(part, axis=1, keepdims=True) * math.log(2.0), (1, 128)
            )
            red_dp[rank, 1:2, :] = jnp.broadcast_to(jnp.sum(w, axis=1, keepdims=True), (1, 128))

            def dp_send_to(r):
                return pltpu.make_async_remote_copy(
                    src_ref=red_dp.at[rank], dst_ref=red_dp.at[rank], send_sem=dp_send.at[r],
                    recv_sem=dp_recv.at[rank], device_id=at_rank(r), device_id_type=MESH,
                )

            def dp_from(r):
                return pltpu.make_async_remote_copy(
                    src_ref=red_dp.at[rank], dst_ref=red_dp.at[r], send_sem=dp_send.at[r],
                    recv_sem=dp_recv.at[r], device_id=at_rank(r), device_id_type=MESH,
                )

            loop(0, rank, lambda r: dp_send_to(r).start())
        a = m + jnp.log2(l / w)
        acol[r * n : (r + 1) * n, :] = jnp.broadcast_to(a, (128, n)).T

    b_rows = [brow[0:1, c * 128 : (c + 1) * 128] for c in range(chunks)]

    def gradients(slot):
        def step(i, carry):
            rows = pl.ds(pl.multiple_of(slot * n + i * CHUNK, CHUNK), CHUNK)
            a = acol[rows, :]
            w2 = 2.0 * wcol[rows, :]
            p = pcol[rows, :]
            for c in range(chunks):
                t = t_all[rows, c * 128 : (c + 1) * 128]
                g = jnp.exp2(t - a) + jnp.exp2(t - b_rows[c])
                g = g - jnp.where(p == ids[c], w2, 0.0)
                g_all[rows, c * 128 : (c + 1) * 128] = g.astype(BF16)
            return carry

        lax.fori_loop(0, steps, step, 0, unroll=True)

    def user_part(slot):
        return jnp.dot(
            g_all[slot * n : (slot + 1) * n, :], i_all[...], preferred_element_type=F32
        )

    def item_part(slot):
        return dot_tn(g_all[:, slot * n : (slot + 1) * n], u_all[...])

    gradients(2)
    far[...] = user_part(2).astype(BF16)
    gu_fr = start(remote(far.at[pl.ds(0, half)], far_right, GU_FAR_RIGHT, right))
    gu_fl = start(remote(far.at[pl.ds(half, half)], far_left, GU_FAR_LEFT, left))
    gradients(1)
    own_gu[...] = user_part(1)
    to_left[0:half, :] = own_gu[0:half, :].astype(BF16)
    gu_l0 = start(remote(to_left.at[pl.ds(0, half)], from_right.at[pl.ds(0, half)], GU_LEFT_0, left))
    gradients(3)
    own_gi[...] = user_part(3)
    to_right[half:n, :] = own_gi[half:n, :].astype(BF16)
    gu_r1 = start(
        remote(to_right.at[pl.ds(half, half)], from_left.at[pl.ds(half, half)], GU_RIGHT_1, right)
    )
    gradients(0)
    core_1[...] = item_part(3).astype(BF16)
    gi_c1 = start(remote(core_1, got_core_1, GI_CORE_1, at_yc(1)))
    core_0[...] = item_part(1).astype(BF16)
    gi_c0 = start(remote(core_0, got_core_0, GI_CORE_0, at_yc(1)))
    other_gi[...] = item_part(2)
    gi_c1.wait_recv()
    to_y[...] = (other_gi[...] + got_core_1[...].astype(F32)).astype(BF16)
    gi_y = start(remote(to_y, from_y, GI_Y, at_yc(2)))

    gu_fr.wait_recv()
    to_right[0:half, :] = (own_gi[0:half, :] + far_right[...].astype(F32)).astype(BF16)
    gu_r0 = start(
        remote(to_right.at[pl.ds(0, half)], from_left.at[pl.ds(0, half)], GU_RIGHT_0, right)
    )
    gu_fl.wait_recv()
    to_left[half:n, :] = (own_gu[half:n, :] + far_left[...].astype(F32)).astype(BF16)
    gu_l1 = start(
        remote(to_left.at[pl.ds(half, half)], from_right.at[pl.ds(half, half)], GU_LEFT_1, left)
    )
    own_gu[...] = user_part(0)
    own_gi[...] = item_part(0)
    gi_c0.wait_recv()
    own_gi[...] = own_gi[...] + got_core_0[...].astype(F32)
    gu_l0.wait_recv()
    gu_r1.wait_recv()
    gu_r0.wait_recv()
    gu_l1.wait_recv()
    own_gu[...] = own_gu[...] + from_left[...].astype(F32) + from_right[...].astype(F32)
    gi_y.wait_recv()
    own_gi[...] = own_gi[...] + from_y[...].astype(F32)

    @pl.when(rank < n_dp - 1)
    def _():
        pl.semaphore_wait(hello, n_dp - 1 - rank)

    loop(rank + 1, n_dp, lambda r: dp_send_to(r).start())
    loop(0, rank, lambda r: dp_from(r).wait_recv())
    loop(rank + 1, n_dp, lambda r: dp_from(r).wait_recv())
    red_blk[0] = jnp.sum(red_dp[...], axis=0)

    def blk_copy(d):
        return pltpu.make_async_remote_copy(
            src_ref=red_blk.at[0], dst_ref=red_blk.at[d], send_sem=blk_send.at[d], recv_sem=blk_recv.at[d],
            device_id={"blk": (me + d) % n_blk, "dp": my_dp}, device_id_type=MESH,
        )

    loop(1, n_blk, lambda d: blk_copy(d).start())
    loop(1, n_blk, lambda d: blk_copy(d).wait_recv())
    sums = jnp.sum(red_blk[...], axis=0)
    weight = sums[1:2, :]
    scale_out[0] = (sums[0:1, :] / weight)[0, 0]
    rows_total = float(n * n_blk * n_dp)
    factor = (rows_total / weight) * (k[:, 0:128] * math.log(2.0))
    factor = jnp.concatenate([factor] * (width // 128), axis=1)
    gu_out[...] = (factor * own_gu[...]).astype(BF16)
    gi_out[...] = (factor * own_gi[...]).astype(BF16)

    for c in started:
        c.wait_send()
    loop(0, rank, lambda r: dp_send_to(r).wait_send())
    loop(rank + 1, n_dp, lambda r: dp_send_to(r).wait_send())
    loop(1, n_blk, lambda d: blk_copy(d).wait_send())


def body(users, items, weights, positives, log_scale):
    users, items = users[0], items[0]
    n, width = users.shape
    n_blk, n_dp = lax.axis_size("blk"), lax.axis_size("dp")
    nyc = 4
    nx = n_blk // nyc
    any_space = pl.BlockSpec(memory_space=pl.ANY)
    vmem = pl.BlockSpec(memory_space=pltpu.VMEM)
    smem = pl.BlockSpec(memory_space=pltpu.SMEM)
    V = pltpu.VMEM
    rows, cols = nx * n, nyc * n
    half = n // 2
    gu, gi, scale = pl.pallas_call(
        functools.partial(kernel, nx, nyc, n_dp, n_blk),
        out_shape=(
            jax.ShapeDtypeStruct((n, width), BF16),
            jax.ShapeDtypeStruct((n, width), BF16),
            jax.ShapeDtypeStruct((1,), F32),
        ),
        in_specs=[any_space, any_space, any_space, any_space, smem],
        out_specs=(vmem, vmem, smem),
        scratch_shapes=[
            V((rows, width), BF16),
            V((cols, width), BF16),
            V((1, n), F32),
            V((1, n), jnp.int32),
            V((nx, 8, n), F32),
            V((rows, cols), F32),
            V((rows, cols), BF16),
            V((rows, 128), F32),
            V((rows, 128), F32),
            V((rows, 128), F32),
            V((n, 128), F32),
            V((3, n, 128), F32),
            V((nx, 16, n), F32),
            V((nyc, 24, n), F32),
            V((8, cols), F32),
            V((n, width), BF16),
            V((half, width), BF16),
            V((half, width), BF16),
            V((n, width), BF16),
            V((n, width), BF16),
            V((n, width), BF16),
            V((n, width), BF16),
            V((n, width), F32),
            V((n, width), F32),
            V((n, width), F32),
            V((n, width), BF16),
            V((n, width), BF16),
            V((n, width), BF16),
            V((n, width), BF16),
            V((n, width), BF16),
            V((n, width), BF16),
            V((n_dp, 8, 128), F32),
            V((n_blk, 8, 128), F32),
            pltpu.SemaphoreType.DMA((4,)),
            pltpu.SemaphoreType.DMA((TRANSFERS,)),
            pltpu.SemaphoreType.DMA((TRANSFERS,)),
            pltpu.SemaphoreType.DMA((n_dp,)),
            pltpu.SemaphoreType.DMA((n_dp,)),
            pltpu.SemaphoreType.DMA((n_blk,)),
            pltpu.SemaphoreType.DMA((n_blk,)),
            pltpu.SemaphoreType.REGULAR,
        ],
        compiler_params=pltpu.CompilerParams(
            collective_id=0, has_side_effects=True, vmem_limit_bytes=60 * 1024 * 1024
        ),
        cost_estimate=pl.CostEstimate(
            flops=6 * rows * cols * width, bytes_accessed=4 * n * width * 2,
            transcendentals=4 * rows * cols,
        ),
        name="loss_gradients",
    )(users, items, weights, positives, log_scale)
    return gu[None], gi[None], scale


def solution(mesh):
    placed = (P("dp", "blk", None), P("dp", "blk", None), P("dp", "blk"), P("dp", "blk"), P())
    return jax.shard_map(
        body,
        mesh=mesh,
        in_specs=placed,
        out_specs=(P("dp", "blk", None), P("dp", "blk", None), P()),
        check_vma=False,
    )
```

```python
import functools
import math

import jax
import jax.numpy as jnp
from jax import lax
from jax.experimental import pallas as pl
from jax.experimental.pallas import tpu as pltpu
from jax.sharding import PartitionSpec as P

MESH = pl.DeviceIdType.MESH
F32 = jnp.float32
BF16 = jnp.bfloat16
LOW = -3.0e38
CHUNK = 32

(
    U_RIGHT_0, U_LEFT_1, U_RIGHT_1, U_LEFT_0, U_RELAY_RIGHT, U_RELAY_LEFT,
    I_CORE, I_Y_0, I_Y_1, I_PASS_0, I_PASS_1,
    WP_RIGHT, WP_LEFT, WP_RELAY, RS_1, RS_2, RS_3, CS_1, CS_2, CS_3,
    GU_FAR_RIGHT, GU_FAR_LEFT, GU_RIGHT_0, GU_RIGHT_1, GU_LEFT_0, GU_LEFT_1,
    GI_CORE_0, GI_CORE_1, GI_Y,
    TRANSFERS,
) = range(30)


def dot_nt(a, b):
    return lax.dot_general(a, b, (((1,), (1,)), ((), ())), preferred_element_type=F32)


def dot_tn(a, b):
    return lax.dot_general(a, b, (((0,), (0,)), ((), ())), preferred_element_type=F32)


def fold_rows(block, op):
    total = block[0:8]
    for r in range(8, block.shape[0], 8):
        total = op(total, block[r : r + 8])
    return total


def kernel(
    nx, nyc, n_dp, n_blk,
    users, items, weights, positives, log_scale,
    gu_out, gi_out, scale_out,
    u_all, i_all, w_in, p_in, wp, t_all, g_all, wcol, pcol, acol, row_m, lines,
    rowst, colst, brow,
    far, far_right, far_left, to_left, to_right, from_left, from_right,
    own_gu, own_gi, other_gi, core_0, core_1, got_core_0, got_core_1, to_y, from_y,
    red_z, red_plane, totals,
    local_sem, send, recv, z_send, z_recv, plane_send, plane_recv, all_send, all_recv, ready,
):
    n = users.shape[0]
    width = users.shape[1]
    half = n // 2
    cols = nyc * n
    chunks = cols // 128
    per = n // 128
    steps = n // CHUNK
    me = lax.axis_index("blk")
    my_dp = lax.axis_index("dp")
    x = me // nyc
    yc = me % nyc
    core = yc % 2
    y = yc // 2
    depth = n_dp // 2
    z = my_dp % depth
    high = my_dp // depth

    def at_x(d):
        return {"blk": ((x + d) % nx) * nyc + yc, "dp": my_dp}

    def at_yc(d):
        c = 1 - core if d % 2 else core
        w = 1 - y if d // 2 else y
        return {"blk": x * nyc + w * 2 + c, "dp": my_dp}

    def at_z(to):
        return {"blk": me, "dp": high * depth + to}

    def at_plane(p):
        return {"blk": p % n_blk, "dp": (p // n_blk) * depth}

    other_group = {"blk": me, "dp": (1 - high) * depth + z}

    right, left = at_x(1), at_x(nx - 1)

    def remote(src, dst, number, device):
        return pltpu.make_async_remote_copy(
            src_ref=src, dst_ref=dst, send_sem=send.at[number], recv_sem=recv.at[number],
            device_id=device, device_id_type=MESH,
        )

    def loop(first, last, action):
        def step(d, carry):
            action(d)
            return carry

        lax.fori_loop(first, last, step, 0)

    def greet(semaphore, device):
        pl.semaphore_signal(semaphore, inc=1, device_id=device, device_id_type=MESH)

    barrier = pltpu.get_barrier_semaphore()
    for device in (right, left, at_yc(1), at_yc(2)):
        greet(barrier, device)
    locals_ = [
        pltpu.make_async_copy(src, dst, local_sem.at[i])
        for i, (src, dst) in enumerate(
            [
                (weights, w_in),
                (positives, p_in),
                (users, u_all.at[pl.ds(0, n)]),
                (items, i_all.at[pl.ds(0, n)]),
            ]
        )
    ]
    for c in locals_:
        c.start()

    @pl.when(z == 0)
    def _():
        loop(1, depth, lambda to: greet(barrier, at_z(to)))

        @pl.when(high == 0)
        def _():
            greet(barrier, other_group)

    wp[0] = jnp.zeros((8, n), F32)
    pl.semaphore_wait(barrier, 4 + jnp.where(my_dp == 0, 0, 1))

    def u_rows(slot, h):
        return u_all.at[pl.ds(slot * n + h * half, half)]

    def i_rows(slot, h):
        return i_all.at[pl.ds(slot * n + h * half, half)]

    started = []

    def start(copy):
        copy.start()
        started.append(copy)
        return copy

    def piece(ref, h):
        return ref.at[pl.ds(h * half, half)]

    u_r0 = start(remote(piece(users, 0), u_rows(1, 0), U_RIGHT_0, right))
    u_l1 = start(remote(piece(users, 1), u_rows(3, 1), U_LEFT_1, left))
    i_y0 = start(remote(piece(items, 0), i_rows(2, 0), I_Y_0, at_yc(2)))
    i_core = start(remote(items, i_all.at[pl.ds(n, n)], I_CORE, at_yc(1)))
    locals_[0].wait()
    locals_[1].wait()
    wp[0, 0:1, :] = w_in[...]
    wp[0, 1:2, :] = p_in[...].astype(F32)
    wp_r = start(remote(wp.at[0], wp.at[1], WP_RIGHT, right))
    wp_l = start(remote(wp.at[0], wp.at[3], WP_LEFT, left))
    u_r1 = start(remote(piece(users, 1), u_rows(1, 1), U_RIGHT_1, right))
    u_l0 = start(remote(piece(users, 0), u_rows(3, 0), U_LEFT_0, left))
    i_y1 = start(remote(piece(items, 1), i_rows(2, 1), I_Y_1, at_yc(2)))
    locals_[2].wait()
    locals_[3].wait()

    k = jnp.exp(jnp.full((1, 2 * n), log_scale[0], F32)) * (1.0 / (math.sqrt(width) * math.log(2.0)))

    def scores(slot, h):
        block = dot_nt(u_all[slot * n : (slot + 1) * n, :], i_all[h * 2 * n : (h + 1) * 2 * n, :])
        t_all[slot * n : (slot + 1) * n, h * 2 * n : (h + 1) * 2 * n] = block * k

    lane = lax.broadcasted_iota(jnp.int32, (1, 128), 1)

    def column_ids(c):
        block, part = c // per, c % per
        owner = at_yc(block)["blk"]
        return (owner * n + part * 128 + lane).astype(F32)

    ids = [column_ids(c) for c in range(chunks)]

    def spread(slot):
        wcol[slot * n : (slot + 1) * n, :] = jnp.broadcast_to(wp[slot, 0:1, :], (128, n)).T
        pcol[slot * n : (slot + 1) * n, :] = jnp.broadcast_to(wp[slot, 1:2, :], (128, n)).T

    def statistics(slot):
        def maxima(i, best):
            rows = pl.ds(pl.multiple_of(slot * n + i * CHUNK, CHUNK), CHUNK)
            top = None
            out = []
            for c in range(chunks):
                t = t_all[rows, c * 128 : (c + 1) * 128]
                top = t if top is None else jnp.maximum(top, t)
                out.append(jnp.maximum(best[c], fold_rows(t, jnp.maximum)))
            here = pl.ds(pl.multiple_of(i * CHUNK, CHUNK), CHUNK)
            row_m[here, :] = jnp.broadcast_to(jnp.max(top, axis=1, keepdims=True), (CHUNK, 128))
            return tuple(out)

        best = lax.fori_loop(
            0, steps, maxima, tuple(jnp.full((8, 128), LOW, F32) for _ in range(chunks)), unroll=True
        )
        best = [jnp.max(b, axis=0, keepdims=True) for b in best]

        def sums(i, total):
            rows = pl.ds(pl.multiple_of(slot * n + i * CHUNK, CHUNK), CHUNK)
            here = pl.ds(pl.multiple_of(i * CHUNK, CHUNK), CHUNK)
            m = row_m[here, :]
            p = pcol[rows, :]
            w = wcol[rows, :]
            out = []
            line = None
            for c in range(chunks):
                t = t_all[rows, c * 128 : (c + 1) * 128]
                d = t - m
                e = jnp.exp2(d)
                cd = t - best[c]
                ce = jnp.exp2(cd)
                at = p == ids[c]
                hit = jnp.where(at, t, 0.0)
                new = (e, e * d, hit)
                line = new if line is None else tuple(a + b for a, b in zip(line, new))
                for q, v in enumerate((ce, ce * cd, hit, jnp.where(at, w, 0.0))):
                    out.append(total[4 * c + q] + fold_rows(v, jnp.add))
            for q in range(3):
                lines[q, here, :] = line[q]
            return tuple(out)

        total = lax.fori_loop(
            0, steps, sums, tuple(jnp.zeros((8, 128), F32) for _ in range(4 * chunks)), unroll=True
        )
        total = [jnp.sum(b, axis=0, keepdims=True) for b in total]
        rowst[0, slot : slot + 1, :] = row_m[...].T[0:1, :]
        for q in range(3):
            at = (q + 1) * nx + slot
            rowst[0, at : at + 1, :] = jnp.sum(lines[q].T, axis=0, keepdims=True)
        return best, total

    parts = {}
    spread(0)
    i_core.wait_recv()
    scores(0, 0)
    wp_r.wait_recv()
    wp_relay = start(remote(wp.at[1], wp.at[2], WP_RELAY, right))
    spread(1)
    wp_l.wait_recv()
    spread(3)
    u_r0.wait_recv()
    relay_r = start(remote(u_rows(1, 0), u_rows(2, 0), U_RELAY_RIGHT, right))
    u_l1.wait_recv()
    relay_l = start(remote(u_rows(3, 1), u_rows(2, 1), U_RELAY_LEFT, left))
    i_y0.wait_recv()
    i_p0 = start(remote(i_rows(2, 0), i_rows(3, 0), I_PASS_0, at_yc(1)))
    wp_relay.wait_recv()
    spread(2)
    u_r1.wait_recv()
    scores(1, 0)
    u_l0.wait_recv()
    scores(3, 0)
    i_y1.wait_recv()
    i_p1 = start(remote(i_rows(2, 1), i_rows(3, 1), I_PASS_1, at_yc(1)))
    i_p0.wait_recv()
    i_p1.wait_recv()
    for slot in (0, 1, 3):
        scores(slot, 1)
        parts[slot] = statistics(slot)
    relay_r.wait_recv()
    relay_l.wait_recv()
    scores(2, 0)
    scores(2, 1)
    parts[2] = statistics(2)

    rs_copies = [start(remote(rowst.at[0], rowst.at[d], RS_1 + d - 1, at_x(d))) for d in (2, 1, 3)]
    colst[0] = jnp.zeros((24, n), F32)
    for c in range(chunks):
        b, q = c // per, (c % per) * 128
        ms = [parts[s][0][c] for s in range(nx)]
        m = functools.reduce(jnp.maximum, ms)
        l = e = 0.0
        for s in range(nx):
            scale = jnp.exp2(ms[s] - m)
            part_l = parts[s][1][4 * c]
            l = l + scale * part_l
            e = e + scale * (parts[s][1][4 * c + 1] + (ms[s] - m) * part_l)
        hit = sum(parts[s][1][4 * c + 2] for s in range(nx))
        cw = sum(parts[s][1][4 * c + 3] for s in range(nx))
        for i, v in enumerate((m, l, e, hit, cw)):
            colst[0, i * nyc + b : i * nyc + b + 1, q : q + 128] = v
    cs_copies = [start(remote(colst.at[0], colst.at[d], CS_1 + d - 1, at_yc(d))) for d in (3, 2, 1)]

    def combine(source, at, count):
        def rows(i):
            return [source[d, i * count + at[d] : i * count + at[d] + 1, :] for d in range(count)]

        ms, ls, es, hits = rows(0), rows(1), rows(2), rows(3)
        m = functools.reduce(jnp.maximum, ms)
        scales = [jnp.exp2(mi - m) for mi in ms]
        l = sum(li * si for li, si in zip(ls, scales))

        def share():
            e = sum(si * (ei + (mi - m) * li) for mi, li, ei, si in zip(ms, ls, es, scales))
            return e / l - (sum(hits) - m)

        return m, l, share

    def column_stats(b):
        at = [b ^ d for d in range(nyc)]
        w = sum(colst[d, 4 * nyc + at[d] : 4 * nyc + at[d] + 1, :] for d in range(nyc))
        return combine(colst, at, nyc) + (w,)

    def row_stats(r):
        return combine(rowst, [(r - d) % nx for d in range(nx)], nx) + (wp[r, 0:1, :],)

    for c in cs_copies:
        c.wait_recv()
    column_0 = column_stats(0)
    part = column_0[3] * column_0[2]()
    for c in rs_copies:
        c.wait_recv()
    row_0 = row_stats(0)
    part = part + row_0[3] * row_0[2]()

    red_z[z] = jnp.zeros((8, 128), F32)
    red_z[z, 0:1, :] = jnp.broadcast_to(jnp.sum(part, axis=1, keepdims=True) * math.log(2.0), (1, 128))
    red_z[z, 1:2, :] = jnp.broadcast_to(jnp.sum(row_0[3], axis=1, keepdims=True), (1, 128))

    def z_copy(source, to):
        return pltpu.make_async_remote_copy(
            src_ref=red_z.at[source], dst_ref=red_z.at[source], send_sem=z_send.at[0],
            recv_sem=z_recv.at[source], device_id=at_z(to), device_id_type=MESH,
        )

    @pl.when(z > 0)
    def _():
        z_copy(z, 0).start()

    @pl.when((z == 0) & (high == 1))
    def _():
        greet(ready, other_group)

    for b in range(nyc):
        m, l, _, w = column_stats(b) if b else column_0
        brow[0:1, b * n : (b + 1) * n] = m + jnp.log2(l / w)
    for r in (2, 1, 3, 0):
        m, l, _, w = row_stats(r) if r else row_0
        acol[r * n : (r + 1) * n, :] = jnp.broadcast_to(m + jnp.log2(l / w), (128, n)).T

    b_rows = [brow[0:1, c * 128 : (c + 1) * 128] for c in range(chunks)]

    def gradients(slot):
        def step(i, carry):
            rows = pl.ds(pl.multiple_of(slot * n + i * CHUNK, CHUNK), CHUNK)
            a = acol[rows, :]
            w2 = 2.0 * wcol[rows, :]
            p = pcol[rows, :]
            for c in range(chunks):
                t = t_all[rows, c * 128 : (c + 1) * 128]
                g = jnp.exp2(t - a) + jnp.exp2(t - b_rows[c])
                g = g - jnp.where(p == ids[c], w2, 0.0)
                g_all[rows, c * 128 : (c + 1) * 128] = g.astype(BF16)
            return carry

        lax.fori_loop(0, steps, step, 0, unroll=True)

    def user_part(slot):
        return jnp.dot(
            g_all[slot * n : (slot + 1) * n, :], i_all[...], preferred_element_type=F32
        )

    def item_part(slot):
        return dot_tn(g_all[:, slot * n : (slot + 1) * n], u_all[...])

    gradients(2)
    far[...] = user_part(2).astype(BF16)
    gu_fr = start(remote(far.at[pl.ds(0, half)], far_right, GU_FAR_RIGHT, right))
    gu_fl = start(remote(far.at[pl.ds(half, half)], far_left, GU_FAR_LEFT, left))
    gradients(1)
    own_gu[...] = user_part(1)
    to_left[0:half, :] = own_gu[0:half, :].astype(BF16)
    gu_l0 = start(remote(to_left.at[pl.ds(0, half)], from_right.at[pl.ds(0, half)], GU_LEFT_0, left))
    gradients(3)
    own_gi[...] = user_part(3)
    to_right[half:n, :] = own_gi[half:n, :].astype(BF16)
    gu_r1 = start(
        remote(to_right.at[pl.ds(half, half)], from_left.at[pl.ds(half, half)], GU_RIGHT_1, right)
    )
    gradients(0)
    core_1[...] = item_part(3).astype(BF16)
    gi_c1 = start(remote(core_1, got_core_1, GI_CORE_1, at_yc(1)))
    core_0[...] = item_part(1).astype(BF16)
    gi_c0 = start(remote(core_0, got_core_0, GI_CORE_0, at_yc(1)))
    other_gi[...] = item_part(2)
    gi_c1.wait_recv()
    to_y[...] = (other_gi[...] + got_core_1[...].astype(F32)).astype(BF16)
    gi_y = start(remote(to_y, from_y, GI_Y, at_yc(2)))

    gu_fr.wait_recv()
    to_right[0:half, :] = (own_gi[0:half, :] + far_right[...].astype(F32)).astype(BF16)
    gu_r0 = start(
        remote(to_right.at[pl.ds(0, half)], from_left.at[pl.ds(0, half)], GU_RIGHT_0, right)
    )
    gu_fl.wait_recv()
    to_left[half:n, :] = (own_gu[half:n, :] + far_left[...].astype(F32)).astype(BF16)
    gu_l1 = start(
        remote(to_left.at[pl.ds(half, half)], from_right.at[pl.ds(half, half)], GU_LEFT_1, left)
    )
    own_gu[...] = user_part(0)
    own_gi[...] = item_part(0)
    gi_c0.wait_recv()
    own_gi[...] = own_gi[...] + got_core_0[...].astype(F32)
    gu_l0.wait_recv()
    gu_r1.wait_recv()
    gu_r0.wait_recv()
    gu_l1.wait_recv()
    own_gu[...] = own_gu[...] + from_left[...].astype(F32) + from_right[...].astype(F32)
    gi_y.wait_recv()
    own_gi[...] = own_gi[...] + from_y[...].astype(F32)

    def plane_copy(source, to):
        return pltpu.make_async_remote_copy(
            src_ref=red_plane.at[source], dst_ref=red_plane.at[source], send_sem=plane_send.at[to],
            recv_sem=plane_recv.at[source], device_id=at_plane(to), device_id_type=MESH,
        )

    def all_copy(to):
        return pltpu.make_async_remote_copy(
            src_ref=totals, dst_ref=totals, send_sem=all_send.at[to], recv_sem=all_recv.at[0],
            device_id=at_z(to), device_id_type=MESH,
        )

    @pl.when(z == 0)
    def _():
        here = high * n_blk + me
        pl.semaphore_wait(ready, 1)

        @pl.when(high == 0)
        def _():
            greet(ready, other_group)

        loop(1, depth, lambda source: z_copy(source, 0).wait_recv())
        red_plane[here] = jnp.sum(red_z[...], axis=0)
        loop(0, here, lambda to: plane_copy(here, to).start())
        loop(here + 1, 2 * n_blk, lambda to: plane_copy(here, to).start())
        loop(0, here, lambda source: plane_copy(source, source).wait_recv())
        loop(here + 1, 2 * n_blk, lambda source: plane_copy(source, source).wait_recv())
        totals[...] = jnp.sum(red_plane[...], axis=0)
        loop(1, depth, lambda to: all_copy(to).start())
        loop(0, here, lambda to: plane_copy(here, to).wait_send())
        loop(here + 1, 2 * n_blk, lambda to: plane_copy(here, to).wait_send())
        loop(1, depth, lambda to: all_copy(to).wait_send())

    @pl.when(z > 0)
    def _():
        all_copy(0).wait_recv()
        z_copy(z, 0).wait_send()

    sums = totals[...]
    weight = sums[1:2, :]
    scale_out[0] = (sums[0:1, :] / weight)[0, 0]
    rows_total = float(n * n_blk * n_dp)
    factor = (rows_total / weight) * (k[:, 0:128] * math.log(2.0))
    factor = jnp.concatenate([factor] * (width // 128), axis=1)
    gu_out[...] = (factor * own_gu[...]).astype(BF16)
    gi_out[...] = (factor * own_gi[...]).astype(BF16)

    for c in started:
        c.wait_send()


def body(users, items, weights, positives, log_scale):
    users, items = users[0], items[0]
    n, width = users.shape
    n_blk, n_dp = lax.axis_size("blk"), lax.axis_size("dp")
    nyc = 4
    nx = n_blk // nyc
    any_space = pl.BlockSpec(memory_space=pl.ANY)
    vmem = pl.BlockSpec(memory_space=pltpu.VMEM)
    smem = pl.BlockSpec(memory_space=pltpu.SMEM)
    V = pltpu.VMEM
    rows, cols = nx * n, nyc * n
    half = n // 2
    gu, gi, scale = pl.pallas_call(
        functools.partial(kernel, nx, nyc, n_dp, n_blk),
        out_shape=(
            pltpu.VMEM((n, width), BF16),
            pltpu.VMEM((n, width), BF16),
            jax.ShapeDtypeStruct((1,), F32),
        ),
        in_specs=[any_space, any_space, any_space, any_space, smem],
        out_specs=(vmem, vmem, smem),
        scratch_shapes=[
            V((rows, width), BF16),
            V((cols, width), BF16),
            V((1, n), F32),
            V((1, n), jnp.int32),
            V((nx, 8, n), F32),
            V((rows, cols), F32),
            V((rows, cols), BF16),
            V((rows, 128), F32),
            V((rows, 128), F32),
            V((rows, 128), F32),
            V((n, 128), F32),
            V((3, n, 128), F32),
            V((nx, 16, n), F32),
            V((nyc, 24, n), F32),
            V((8, cols), F32),
            V((n, width), BF16),
            V((half, width), BF16),
            V((half, width), BF16),
            V((n, width), BF16),
            V((n, width), BF16),
            V((n, width), BF16),
            V((n, width), BF16),
            V((n, width), F32),
            V((n, width), F32),
            V((n, width), F32),
            V((n, width), BF16),
            V((n, width), BF16),
            V((n, width), BF16),
            V((n, width), BF16),
            V((n, width), BF16),
            V((n, width), BF16),
            V((n_dp // 2, 8, 128), F32),
            V((2 * n_blk, 8, 128), F32),
            V((8, 128), F32),
            pltpu.SemaphoreType.DMA((4,)),
            pltpu.SemaphoreType.DMA((TRANSFERS,)),
            pltpu.SemaphoreType.DMA((TRANSFERS,)),
            pltpu.SemaphoreType.DMA((1,)),
            pltpu.SemaphoreType.DMA((n_dp // 2,)),
            pltpu.SemaphoreType.DMA((2 * n_blk,)),
            pltpu.SemaphoreType.DMA((2 * n_blk,)),
            pltpu.SemaphoreType.DMA((n_dp // 2,)),
            pltpu.SemaphoreType.DMA((1,)),
            pltpu.SemaphoreType.REGULAR,
        ],
        compiler_params=pltpu.CompilerParams(
            collective_id=0, has_side_effects=True, vmem_limit_bytes=60 * 1024 * 1024
        ),
        cost_estimate=pl.CostEstimate(
            flops=6 * rows * cols * width, bytes_accessed=4 * n * width * 2,
            transcendentals=4 * rows * cols,
        ),
        name="loss_gradients",
    )(users, items, weights, positives, log_scale)
    return gu[None], gi[None], scale


def solution(mesh):
    placed = (P("dp", "blk", None), P("dp", "blk", None), P("dp", "blk"), P("dp", "blk"), P())
    return jax.shard_map(
        body,
        mesh=mesh,
        in_specs=placed,
        out_specs=(P("dp", "blk", None), P("dp", "blk", None), P()),
        check_vma=False,
    )
```

```python
import functools
import math

import jax
import jax.numpy as jnp
from jax import lax
from jax.experimental import pallas as pl
from jax.experimental.pallas import tpu as pltpu
from jax.sharding import PartitionSpec as P

MESH = pl.DeviceIdType.MESH
F32 = jnp.float32
BF16 = jnp.bfloat16
LOW = -3.0e38
CHUNK = 32

(
    U_RIGHT_0, U_LEFT_1, U_RIGHT_1, U_LEFT_0, U_RELAY_RIGHT, U_RELAY_LEFT,
    I_CORE, I_Y, I_Y_1, I_Y_2, I_Y_3, I_PASS, I_PASS_1, I_PASS_2, I_PASS_3,
    WP_RIGHT, WP_LEFT, WP_RELAY, RS_1, RS_2, RS_3, CS_1, CS_2, CS_3, RO_1, RO_2, RO_3, CO_1, CO_2, CO_3,
    GU_FAR_RIGHT, GU_FAR_LEFT, GU_RIGHT_0, GU_RIGHT_1, GU_LEFT_0, GU_LEFT_1,
    GI_CORE_0, GI_CORE_1, GI_Y,
    TRANSFERS,
) = range(40)


def dot_nt(a, b):
    return lax.dot_general(a, b, (((1,), (1,)), ((), ())), preferred_element_type=F32)


def dot_tn(a, b):
    return lax.dot_general(a, b, (((0,), (0,)), ((), ())), preferred_element_type=F32)


def fold_rows(block, op):
    total = block[0:8]
    for r in range(8, block.shape[0], 8):
        total = op(total, block[r : r + 8])
    return total


def kernel(
    nx, nyc, n_dp, n_blk,
    users, items, weights, positives, log_scale,
    gu_out, gi_out, scale_out, factor_out,
    u_all, i_all, w_in, p_in, wp, t_all, g_all, wcol, pcol, acol, row_m, lines,
    rowst, colst, row_own, col_own, log_in,
    far, far_right, far_left, to_left, to_right, from_left, from_right,
    own_gu, own_gi, other_gi, core_0, core_1, got_core_0, got_core_1, to_y, from_y,
    red_z, red_plane, totals,
    local_sem, send, recv, z_send, z_recv, plane_send, plane_recv, all_send, all_recv, ready,
):
    n = users.shape[0]
    width = users.shape[1]
    half = n // 2
    cols = nyc * n
    chunks = cols // 128
    per = n // 128
    steps = n // CHUNK
    me = lax.axis_index("blk")
    my_dp = lax.axis_index("dp")
    x = me // nyc
    yc = me % nyc
    core = yc % 2
    y = yc // 2
    depth = n_dp // 2
    z = my_dp % depth
    high = my_dp // depth

    def at_x(d):
        return {"blk": ((x + d) % nx) * nyc + yc, "dp": my_dp}

    def at_yc(d):
        c = 1 - core if d % 2 else core
        w = 1 - y if d // 2 else y
        return {"blk": x * nyc + w * 2 + c, "dp": my_dp}

    def at_z(to):
        return {"blk": me, "dp": high * depth + to}

    def at_plane(p):
        return {"blk": p % n_blk, "dp": (p // n_blk) * depth}

    other_group = {"blk": me, "dp": (1 - high) * depth + z}

    right, left = at_x(1), at_x(nx - 1)

    def remote(src, dst, number, device):
        return pltpu.make_async_remote_copy(
            src_ref=src, dst_ref=dst, send_sem=send.at[number], recv_sem=recv.at[number],
            device_id=device, device_id_type=MESH,
        )

    def loop(first, last, action):
        def step(d, carry):
            action(d)
            return carry

        lax.fori_loop(first, last, step, 0)

    def greet(semaphore, device):
        pl.semaphore_signal(semaphore, inc=1, device_id=device, device_id_type=MESH)

    barrier = pltpu.get_barrier_semaphore()
    for device in (right, left, at_yc(1), at_yc(2)):
        greet(barrier, device)
    locals_ = [
        pltpu.make_async_copy(src, dst, local_sem.at[i])
        for i, (src, dst) in enumerate(
            [
                (weights, w_in),
                (positives, p_in),
                (users, u_all.at[pl.ds(0, n)]),
                (items, i_all.at[pl.ds(0, n)]),
                (log_scale, log_in),
            ]
        )
    ]
    for c in locals_:
        c.start()

    @pl.when(z == 0)
    def _():
        loop(1, depth, lambda to: greet(barrier, at_z(to)))

        @pl.when(high == 0)
        def _():
            greet(barrier, other_group)

    wp[0] = jnp.zeros((8, n), F32)
    col_own[0:nyc] = jnp.zeros((nyc, 16, 128), F32)
    pl.semaphore_wait(barrier, 4 + jnp.where(my_dp == 0, 0, 1))

    def u_rows(slot, h):
        return u_all.at[pl.ds(slot * n + h * half, half)]

    quarter = n // 4

    def i_rows(slot, q):
        return i_all.at[pl.ds(slot * n + q * quarter, quarter)]

    started = []

    def start(copy):
        copy.start()
        started.append(copy)
        return copy

    def piece(ref, h):
        return ref.at[pl.ds(h * half, half)]

    u_r0 = start(remote(piece(users, 0), u_rows(1, 0), U_RIGHT_0, right))
    u_l1 = start(remote(piece(users, 1), u_rows(3, 1), U_LEFT_1, left))
    i_y = [
        start(remote(items.at[pl.ds(q * quarter, quarter)], i_rows(2, q), I_Y + q, at_yc(2)))
        for q in range(4)
    ]
    i_core = start(remote(items, i_all.at[pl.ds(n, n)], I_CORE, at_yc(1)))
    locals_[0].wait()
    locals_[1].wait()
    wp[0, 0:1, :] = w_in[...]
    wp[0, 1:2, :] = p_in[...].astype(F32)
    wp_r = start(remote(wp.at[0], wp.at[1], WP_RIGHT, right))
    wp_l = start(remote(wp.at[0], wp.at[3], WP_LEFT, left))
    u_r1 = start(remote(piece(users, 1), u_rows(1, 1), U_RIGHT_1, right))
    u_l0 = start(remote(piece(users, 0), u_rows(3, 0), U_LEFT_0, left))
    for c in locals_[2:]:
        c.wait()

    k = jnp.exp(jnp.full((1, 2 * n), log_in[0], F32)) * (1.0 / (math.sqrt(width) * math.log(2.0)))

    def scores(slot, first, last):
        block = dot_nt(u_all[slot * n : (slot + 1) * n, :], i_all[first * n : last * n, :])
        for b in range(last - first):
            t_all[slot * n : (slot + 1) * n, (first + b) * n : (first + b + 1) * n] = (
                block[:, b * n : (b + 1) * n] * k[:, 0:n]
            )

    lane = lax.broadcasted_iota(jnp.int32, (1, 128), 1)

    def column_ids(c):
        block, part = c // per, c % per
        owner = at_yc(block)["blk"]
        return (owner * n + part * 128 + lane).astype(F32)

    ids = [column_ids(c) for c in range(chunks)]

    def spread(slot):
        wcol[slot * n : (slot + 1) * n, :] = jnp.broadcast_to(wp[slot, 0:1, :], (128, n)).T
        pcol[slot * n : (slot + 1) * n, :] = jnp.broadcast_to(wp[slot, 1:2, :], (128, n)).T

    def statistics(slot):
        def maxima(i, best):
            rows = pl.ds(pl.multiple_of(slot * n + i * CHUNK, CHUNK), CHUNK)
            top = None
            out = []
            for c in range(chunks):
                t = t_all[rows, c * 128 : (c + 1) * 128]
                top = t if top is None else jnp.maximum(top, t)
                out.append(jnp.maximum(best[c], fold_rows(t, jnp.maximum)))
            here = pl.ds(pl.multiple_of(i * CHUNK, CHUNK), CHUNK)
            row_m[here, :] = jnp.broadcast_to(jnp.max(top, axis=1, keepdims=True), (CHUNK, 128))
            return tuple(out)

        best = lax.fori_loop(
            0, steps, maxima, tuple(jnp.full((8, 128), LOW, F32) for _ in range(chunks)), unroll=True
        )
        best = [jnp.max(b, axis=0, keepdims=True) for b in best]

        def sums(i, total):
            rows = pl.ds(pl.multiple_of(slot * n + i * CHUNK, CHUNK), CHUNK)
            here = pl.ds(pl.multiple_of(i * CHUNK, CHUNK), CHUNK)
            m = row_m[here, :]
            p = pcol[rows, :]
            w = wcol[rows, :]
            out = []
            line = None
            for c in range(chunks):
                t = t_all[rows, c * 128 : (c + 1) * 128]
                d = t - m
                e = jnp.exp2(d)
                cd = t - best[c]
                ce = jnp.exp2(cd)
                at = p == ids[c]
                hit = jnp.where(at, t, 0.0)
                new = (e, e * d, hit)
                line = new if line is None else tuple(a + b for a, b in zip(line, new))
                for q, v in enumerate((ce, ce * cd, hit, jnp.where(at, w, 0.0))):
                    out.append(total[4 * c + q] + fold_rows(v, jnp.add))
            for q in range(3):
                lines[q, here, :] = line[q]
            return tuple(out)

        total = lax.fori_loop(
            0, steps, sums, tuple(jnp.zeros((8, 128), F32) for _ in range(4 * chunks)), unroll=True
        )
        total = [jnp.sum(b, axis=0, keepdims=True) for b in total]
        row = [row_m[...].T[0:1, :]] + [jnp.sum(lines[q].T, axis=0, keepdims=True) for q in range(3)]
        for q in range(4):
            for h in range(per):
                v = row[q][:, h * 128 : (h + 1) * 128]
                row_own[nx - slot, q * per + h : q * per + h + 1, :] = v
                if q < 2:
                    at = (q * nx + slot) * per + h
                    rowst[0, at : at + 1, :] = v
        return best, total

    parts = {}
    spread(0)
    i_core.wait_recv()
    scores(0, 0, 2)
    wp_r.wait_recv()
    wp_relay = start(remote(wp.at[1], wp.at[2], WP_RELAY, right))
    spread(1)
    wp_l.wait_recv()
    spread(3)

    i_pass = []

    def pass_on(q):
        i_y[q].wait_recv()
        i_pass.append(start(remote(i_rows(2, q), i_rows(3, q), I_PASS + q, at_yc(1))))

    pass_on(0)
    u_r0.wait_recv()
    relay_r = start(remote(u_rows(1, 0), u_rows(2, 0), U_RELAY_RIGHT, right))
    u_l1.wait_recv()
    relay_l = start(remote(u_rows(3, 1), u_rows(2, 1), U_RELAY_LEFT, left))
    pass_on(1)
    wp_relay.wait_recv()
    spread(2)
    pass_on(2)
    pass_on(3)
    scores(0, 2, 3)
    u_r1.wait_recv()
    scores(1, 0, 3)
    u_l0.wait_recv()
    scores(3, 0, 3)
    for c in i_pass:
        c.wait_recv()
    for slot in (0, 1, 3):
        scores(slot, 3, 4)
        parts[slot] = statistics(slot)
    relay_r.wait_recv()
    relay_l.wait_recv()
    scores(2, 0, 4)
    parts[2] = statistics(2)

    ro_copies = [start(remote(row_own.at[d], row_own.at[nx + d], RO_1 + d - 1, at_x(d))) for d in (2, 1, 3)]
    for c in range(chunks):
        b, h = c // per, c % per
        ms = [parts[s][0][c] for s in range(nx)]
        m = functools.reduce(jnp.maximum, ms)
        l = e = 0.0
        for s in range(nx):
            scale = jnp.exp2(ms[s] - m)
            part_l = parts[s][1][4 * c]
            l = l + scale * part_l
            e = e + scale * (parts[s][1][4 * c + 1] + (ms[s] - m) * part_l)
        hit = sum(parts[s][1][4 * c + 2] for s in range(nx))
        cw = sum(parts[s][1][4 * c + 3] for s in range(nx))
        for q, v in enumerate((m, l, e, hit, cw)):
            col_own[b, q * per + h : q * per + h + 1, :] = v
        for q, v in enumerate((m, l, cw)):
            at = (q * nyc + b) * per + h
            colst[0, at : at + 1, :] = v
    co_copies = [start(remote(col_own.at[d], col_own.at[nyc + d], CO_1 + d - 1, at_yc(d))) for d in (3, 2, 1)]
    rs_copies = [start(remote(rowst.at[0], rowst.at[d], RS_1 + d - 1, at_x(d))) for d in (2, 1, 3)]
    cs_copies = [start(remote(colst.at[0], colst.at[d], CS_1 + d - 1, at_yc(d))) for d in (3, 2, 1)]

    def total_share(sources, w):
        ms, ls, es, hits = ([src(q) for src in sources] for q in range(4))
        m = functools.reduce(jnp.maximum, ms)
        scales = [jnp.exp2(mi - m) for mi in ms]
        l = sum(li * si for li, si in zip(ls, scales))
        e = sum(si * (ei + (mi - m) * li) for mi, li, ei, si in zip(ms, ls, es, scales))
        return w * (e / l - (sum(hits) - m))

    def own_rows(ref, i):
        return lambda q: ref[i, q * per : (q + 1) * per, :]

    for c in co_copies:
        c.wait_recv()
    columns = [own_rows(col_own, i) for i in [0] + [nyc + d for d in range(1, nyc)]]
    part = total_share(columns, sum(src(4) for src in columns))
    for c in ro_copies:
        c.wait_recv()
    w_own = jnp.concatenate([wp[0, 0:1, h * 128 : (h + 1) * 128] for h in range(per)], axis=0)
    part = part + total_share([own_rows(row_own, nx + d) for d in range(nx)], w_own)

    def line(v):
        v = jnp.sum(jnp.sum(v, axis=0, keepdims=True), axis=1, keepdims=True)
        return jnp.broadcast_to(v, (1, 128))

    red_z[z] = jnp.zeros((8, 128), F32)
    red_z[z, 0:1, :] = line(part) * math.log(2.0)
    red_z[z, 1:2, :] = line(w_own)

    def z_copy(source, to):
        return pltpu.make_async_remote_copy(
            src_ref=red_z.at[source], dst_ref=red_z.at[source], send_sem=z_send.at[0],
            recv_sem=z_recv.at[source], device_id=at_z(to), device_id_type=MESH,
        )

    @pl.when(z > 0)
    def _():
        z_copy(z, 0).start()

    @pl.when((z == 0) & (high == 1))
    def _():
        greet(ready, other_group)

    def exponent(ref, at, count, w):
        ms, ls = (
            [ref[d, (q * count + at[d]) * per : (q * count + at[d] + 1) * per, :] for d in range(count)]
            for q in range(2)
        )
        m = functools.reduce(jnp.maximum, ms)
        l = sum(li * jnp.exp2(mi - m) for mi, li in zip(ms, ls))
        return m + jnp.log2(l / w)

    for c in cs_copies:
        c.wait_recv()
    b_rows = []
    for b in range(nyc):
        at = [b ^ d for d in range(nyc)]
        w = sum(colst[d, (2 * nyc + at[d]) * per : (2 * nyc + at[d] + 1) * per, :] for d in range(nyc))
        v = exponent(colst, at, nyc, w)
        b_rows += [v[h : h + 1, :] for h in range(per)]
    for c in rs_copies:
        c.wait_recv()
    for r in (2, 1, 3, 0):
        w = jnp.concatenate([wp[r, 0:1, h * 128 : (h + 1) * 128] for h in range(per)], axis=0)
        a = exponent(rowst, [(r - d) % nx for d in range(nx)], nx, w)
        for h in range(per):
            acol[r * n + h * 128 : r * n + (h + 1) * 128, :] = jnp.broadcast_to(a[h : h + 1, :], (128, 128)).T

    def gradients(slot):
        def step(i, carry):
            rows = pl.ds(pl.multiple_of(slot * n + i * CHUNK, CHUNK), CHUNK)
            a = acol[rows, :]
            w2 = 2.0 * wcol[rows, :]
            p = pcol[rows, :]
            for c in range(chunks):
                t = t_all[rows, c * 128 : (c + 1) * 128]
                g = jnp.exp2(t - a) + jnp.exp2(t - b_rows[c])
                g = g - jnp.where(p == ids[c], w2, 0.0)
                g_all[rows, c * 128 : (c + 1) * 128] = g.astype(BF16)
            return carry

        lax.fori_loop(0, steps, step, 0, unroll=True)

    def user_part(slot):
        return jnp.dot(
            g_all[slot * n : (slot + 1) * n, :], i_all[...], preferred_element_type=F32
        )

    def item_part(slot):
        return dot_tn(g_all[:, slot * n : (slot + 1) * n], u_all[...])

    gradients(2)
    far[...] = user_part(2).astype(BF16)
    gu_fr = start(remote(far.at[pl.ds(0, half)], far_right, GU_FAR_RIGHT, right))
    gu_fl = start(remote(far.at[pl.ds(half, half)], far_left, GU_FAR_LEFT, left))
    gradients(1)
    own_gu[...] = user_part(1)
    to_left[0:half, :] = own_gu[0:half, :].astype(BF16)
    gu_l0 = start(remote(to_left.at[pl.ds(0, half)], from_right.at[pl.ds(0, half)], GU_LEFT_0, left))
    gradients(3)
    own_gi[...] = user_part(3)
    to_right[half:n, :] = own_gi[half:n, :].astype(BF16)
    gu_r1 = start(
        remote(to_right.at[pl.ds(half, half)], from_left.at[pl.ds(half, half)], GU_RIGHT_1, right)
    )
    gradients(0)
    core_1[...] = item_part(3).astype(BF16)
    gi_c1 = start(remote(core_1, got_core_1, GI_CORE_1, at_yc(1)))
    core_0[...] = item_part(1).astype(BF16)
    gi_c0 = start(remote(core_0, got_core_0, GI_CORE_0, at_yc(1)))
    other_gi[...] = item_part(2)
    gi_c1.wait_recv()
    to_y[...] = (other_gi[...] + got_core_1[...].astype(F32)).astype(BF16)
    gi_y = start(remote(to_y, from_y, GI_Y, at_yc(2)))

    gu_fr.wait_recv()
    to_right[0:half, :] = (own_gi[0:half, :] + far_right[...].astype(F32)).astype(BF16)
    gu_r0 = start(
        remote(to_right.at[pl.ds(0, half)], from_left.at[pl.ds(0, half)], GU_RIGHT_0, right)
    )
    gu_fl.wait_recv()
    to_left[half:n, :] = (own_gu[half:n, :] + far_left[...].astype(F32)).astype(BF16)
    gu_l1 = start(
        remote(to_left.at[pl.ds(half, half)], from_right.at[pl.ds(half, half)], GU_LEFT_1, left)
    )
    own_gu[...] = user_part(0)
    own_gi[...] = item_part(0)
    gi_c0.wait_recv()
    own_gi[...] = own_gi[...] + got_core_0[...].astype(F32)
    gu_l0.wait_recv()
    gu_r1.wait_recv()
    gu_r0.wait_recv()
    gu_l1.wait_recv()
    gu_out[...] = own_gu[...] + from_left[...].astype(F32) + from_right[...].astype(F32)
    gi_y.wait_recv()
    gi_out[...] = own_gi[...] + from_y[...].astype(F32)

    def plane_copy(source, to):
        return pltpu.make_async_remote_copy(
            src_ref=red_plane.at[source], dst_ref=red_plane.at[source], send_sem=plane_send.at[to],
            recv_sem=plane_recv.at[source], device_id=at_plane(to), device_id_type=MESH,
        )

    def all_copy(to):
        return pltpu.make_async_remote_copy(
            src_ref=totals, dst_ref=totals, send_sem=all_send.at[to], recv_sem=all_recv.at[0],
            device_id=at_z(to), device_id_type=MESH,
        )

    @pl.when(z == 0)
    def _():
        here = high * n_blk + me
        pl.semaphore_wait(ready, 1)

        @pl.when(high == 0)
        def _():
            greet(ready, other_group)

        loop(1, depth, lambda source: z_copy(source, 0).wait_recv())
        red_plane[here] = jnp.sum(red_z[...], axis=0)
        loop(0, here, lambda to: plane_copy(here, to).start())
        loop(here + 1, 2 * n_blk, lambda to: plane_copy(here, to).start())
        loop(0, here, lambda source: plane_copy(source, source).wait_recv())
        loop(here + 1, 2 * n_blk, lambda source: plane_copy(source, source).wait_recv())
        totals[...] = jnp.sum(red_plane[...], axis=0)
        loop(1, depth, lambda to: all_copy(to).start())

    @pl.when(z > 0)
    def _():
        all_copy(0).wait_recv()

    sums = totals[...]
    weight = sums[1:2, :]
    scale_out[...] = jnp.broadcast_to(sums[0:1, :] / weight, (8, 128))
    rows_total = float(n * n_blk * n_dp)
    factor = (rows_total / weight) * (k[:, 0:128] * math.log(2.0))
    factor_out[...] = jnp.concatenate([factor] * (width // 128), axis=1)

    for c in started:
        c.wait_send()

    @pl.when(z > 0)
    def _():
        z_copy(z, 0).wait_send()

    @pl.when(z == 0)
    def _():
        here = high * n_blk + me
        loop(0, here, lambda to: plane_copy(here, to).wait_send())
        loop(here + 1, 2 * n_blk, lambda to: plane_copy(here, to).wait_send())
        loop(1, depth, lambda to: all_copy(to).wait_send())


def body(users, items, weights, positives, log_scale):
    users, items = users[0], items[0]
    n, width = users.shape
    n_blk, n_dp = lax.axis_size("blk"), lax.axis_size("dp")
    nyc = 4
    nx = n_blk // nyc
    any_space = pl.BlockSpec(memory_space=pl.ANY)
    vmem = pl.BlockSpec(memory_space=pltpu.VMEM)
    V = pltpu.VMEM
    rows, cols = nx * n, nyc * n
    half = n // 2
    gu, gi, scale, factor = pl.pallas_call(
        functools.partial(kernel, nx, nyc, n_dp, n_blk),
        out_shape=(
            V((n, width), F32),
            V((n, width), F32),
            V((8, 128), F32),
            V((1, width), F32),
        ),
        in_specs=[any_space] * 5,
        out_specs=(vmem,) * 4,
        scratch_shapes=[
            V((rows, width), BF16),
            V((cols, width), BF16),
            V((1, n), F32),
            V((1, n), jnp.int32),
            V((nx, 8, n), F32),
            V((rows, cols), F32),
            V((rows, cols), BF16),
            V((rows, 128), F32),
            V((rows, 128), F32),
            V((rows, 128), F32),
            V((n, 128), F32),
            V((3, n, 128), F32),
            V((nx, 2 * nx * n // 128, 128), F32),
            V((nyc, 3 * nyc * n // 128, 128), F32),
            V((2 * nx, 8, 128), F32),
            V((2 * nyc, 16, 128), F32),
            pltpu.SMEM((1,), F32),
            V((n, width), BF16),
            V((half, width), BF16),
            V((half, width), BF16),
            V((n, width), BF16),
            V((n, width), BF16),
            V((n, width), BF16),
            V((n, width), BF16),
            V((n, width), F32),
            V((n, width), F32),
            V((n, width), F32),
            V((n, width), BF16),
            V((n, width), BF16),
            V((n, width), BF16),
            V((n, width), BF16),
            V((n, width), BF16),
            V((n, width), BF16),
            V((n_dp // 2, 8, 128), F32),
            V((2 * n_blk, 8, 128), F32),
            V((8, 128), F32),
            pltpu.SemaphoreType.DMA((5,)),
            pltpu.SemaphoreType.DMA((TRANSFERS,)),
            pltpu.SemaphoreType.DMA((TRANSFERS,)),
            pltpu.SemaphoreType.DMA((1,)),
            pltpu.SemaphoreType.DMA((n_dp // 2,)),
            pltpu.SemaphoreType.DMA((2 * n_blk,)),
            pltpu.SemaphoreType.DMA((2 * n_blk,)),
            pltpu.SemaphoreType.DMA((n_dp // 2,)),
            pltpu.SemaphoreType.DMA((1,)),
            pltpu.SemaphoreType.REGULAR,
        ],
        compiler_params=pltpu.CompilerParams(
            collective_id=0, has_side_effects=True, vmem_limit_bytes=60 * 1024 * 1024
        ),
        cost_estimate=pl.CostEstimate(
            flops=6 * rows * cols * width, bytes_accessed=4 * n * width * 2,
            transcendentals=4 * rows * cols,
        ),
        name="loss_gradients",
    )(users, items, weights, positives, log_scale)
    return (gu * factor).astype(BF16)[None], (gi * factor).astype(BF16)[None], scale[0, 0:1]


def solution(mesh):
    placed = (P("dp", "blk", None), P("dp", "blk", None), P("dp", "blk"), P("dp", "blk"), P())
    return jax.shard_map(
        body,
        mesh=mesh,
        in_specs=placed,
        out_specs=(P("dp", "blk", None), P("dp", "blk", None), P()),
        check_vma=False,
    )
```

```python
import functools
import math

import jax
import jax.numpy as jnp
from jax import lax
from jax.experimental import pallas as pl
from jax.experimental.pallas import tpu as pltpu
from jax.sharding import PartitionSpec as P

MESH = pl.DeviceIdType.MESH
F32 = jnp.float32
BF16 = jnp.bfloat16
LOW = -3.0e38
CHUNK = 32

(
    U_RIGHT_0, U_LEFT_1, U_RIGHT_1, U_LEFT_0, U_RELAY_RIGHT, U_RELAY_LEFT,
    I_CORE, I_Y, I_Y_1, I_Y_2, I_Y_3, I_PASS, I_PASS_1, I_PASS_2, I_PASS_3,
    WP_RIGHT, WP_LEFT, WP_RELAY, RS_1, RS_2, RS_3, CS_1, CS_2, CS_3,
    GU_FAR_RIGHT, GU_FAR_LEFT, GU_RIGHT_0, GU_RIGHT_1, GU_LEFT_0, GU_LEFT_1,
    GI_CORE_0, GI_CORE_1, GI_Y,
    TRANSFERS,
) = range(34)


def dot_nt(a, b):
    return lax.dot_general(a, b, (((1,), (1,)), ((), ())), preferred_element_type=F32)


def dot_tn(a, b):
    return lax.dot_general(a, b, (((0,), (0,)), ((), ())), preferred_element_type=F32)


def fold_rows(block, op):
    total = block[0:8]
    for r in range(8, block.shape[0], 8):
        total = op(total, block[r : r + 8])
    return total


def kernel(
    nx, nyc, n_dp, n_blk,
    users, items, weights, positives, log_scale,
    gu_out, gi_out, scale_out, factor_out,
    u_all, i_all, w_in, p_in, wp, t_all, g_all, wcol, pcol, acol, row_m, lines,
    rowst, colst, log_in,
    far, far_right, far_left, to_left, to_right, from_left, from_right,
    own_gu, own_gi, other_gi, core_0, core_1, got_core_0, got_core_1, to_y, from_y,
    mine, parts_in, totals,
    local_sem, send, recv, part_send, part_recv, all_send, all_recv, hello, ready, go,
):
    n = users.shape[0]
    width = users.shape[1]
    half = n // 2
    cols = nyc * n
    chunks = cols // 128
    per = n // 128
    steps = n // CHUNK
    me = lax.axis_index("blk")
    my_dp = lax.axis_index("dp")
    x = me // nyc
    yc = me % nyc
    core = yc % 2
    y = yc // 2
    depth = n_dp // 2
    z = my_dp % depth
    high = my_dp // depth

    def at_x(d):
        return {"blk": ((x + d) % nx) * nyc + yc, "dp": my_dp}

    def at_yc(d):
        c = 1 - core if d % 2 else core
        w = 1 - y if d // 2 else y
        return {"blk": x * nyc + w * 2 + c, "dp": my_dp}

    def at_z(to):
        return {"blk": me, "dp": high * depth + to}

    def at_plane(r):
        if r < 8:
            flip, dx, c = r % 4, 0, (1 - core if r >= 4 else core)
        else:
            flip, dx, c = (r - 8) // 3, (r - 8) % 3 + 1, core
        w = 1 - y if flip in (1, 2) else y
        v = 1 - high if flip in (1, 3) else high
        return {"blk": ((x + dx) % nx) * nyc + w * 2 + c, "dp": v * depth}

    next_y = at_plane(1)

    right, left = at_x(1), at_x(nx - 1)

    def remote(src, dst, number, device):
        return pltpu.make_async_remote_copy(
            src_ref=src, dst_ref=dst, send_sem=send.at[number], recv_sem=recv.at[number],
            device_id=device, device_id_type=MESH,
        )

    def loop(first, last, action):
        def step(d, carry):
            action(d)
            return carry

        lax.fori_loop(first, last, step, 0)

    def greet(semaphore, device):
        pl.semaphore_signal(semaphore, inc=1, device_id=device, device_id_type=MESH)

    barrier = pltpu.get_barrier_semaphore()
    for device in (right, left, at_yc(1), at_yc(2)):
        greet(barrier, device)
    locals_ = [
        pltpu.make_async_copy(src, dst, local_sem.at[i])
        for i, (src, dst) in enumerate(
            [
                (weights, w_in),
                (positives, p_in),
                (users, u_all.at[pl.ds(0, n)]),
                (items, i_all.at[pl.ds(0, n)]),
                (log_scale, log_in),
            ]
        )
    ]
    for c in locals_:
        c.start()

    @pl.when(z == 0)
    def _():
        loop(1, depth, lambda to: greet(barrier, at_z(to)))

        @pl.when(high == 0)
        def _():
            greet(barrier, next_y)

    wp[0] = jnp.zeros((8, n), F32)
    pl.semaphore_wait(barrier, 4 + jnp.where(my_dp == 0, 0, 1))

    def u_rows(slot, h):
        return u_all.at[pl.ds(slot * n + h * half, half)]

    quarter = n // 4

    def i_rows(slot, q):
        return i_all.at[pl.ds(slot * n + q * quarter, quarter)]

    started = []

    def start(copy):
        copy.start()
        started.append(copy)
        return copy

    def piece(ref, h):
        return ref.at[pl.ds(h * half, half)]

    u_r0 = start(remote(piece(users, 0), u_rows(1, 0), U_RIGHT_0, right))
    u_l1 = start(remote(piece(users, 1), u_rows(3, 1), U_LEFT_1, left))
    i_y = [
        start(remote(items.at[pl.ds(q * quarter, quarter)], i_rows(2, q), I_Y + q, at_yc(2)))
        for q in range(4)
    ]
    i_core = start(remote(items, i_all.at[pl.ds(n, n)], I_CORE, at_yc(1)))
    locals_[0].wait()
    locals_[1].wait()
    wp[0, 0:1, :] = w_in[...]
    wp[0, 1:2, :] = p_in[...].astype(F32)
    wp_r = start(remote(wp.at[0], wp.at[1], WP_RIGHT, right))
    wp_l = start(remote(wp.at[0], wp.at[3], WP_LEFT, left))
    u_r1 = start(remote(piece(users, 1), u_rows(1, 1), U_RIGHT_1, right))
    u_l0 = start(remote(piece(users, 0), u_rows(3, 0), U_LEFT_0, left))
    for c in locals_[2:]:
        c.wait()

    @pl.when(z > 0)
    def _():
        greet(hello, at_z(0))

    k = jnp.exp(jnp.full((1, 2 * n), log_in[0], F32)) * (1.0 / (math.sqrt(width) * math.log(2.0)))

    def scores(slot, first, last):
        block = dot_nt(u_all[slot * n : (slot + 1) * n, :], i_all[first * n : last * n, :])
        for b in range(last - first):
            t_all[slot * n : (slot + 1) * n, (first + b) * n : (first + b + 1) * n] = (
                block[:, b * n : (b + 1) * n] * k[:, 0:n]
            )

    lane = lax.broadcasted_iota(jnp.int32, (1, 128), 1)

    def column_ids(c):
        block, part = c // per, c % per
        owner = at_yc(block)["blk"]
        return (owner * n + part * 128 + lane).astype(F32)

    ids = [column_ids(c) for c in range(chunks)]

    def spread(slot):
        wcol[slot * n : (slot + 1) * n, :] = jnp.broadcast_to(wp[slot, 0:1, :], (128, n)).T
        pcol[slot * n : (slot + 1) * n, :] = jnp.broadcast_to(wp[slot, 1:2, :], (128, n)).T

    def statistics(slot):
        def maxima(i, best):
            rows = pl.ds(pl.multiple_of(slot * n + i * CHUNK, CHUNK), CHUNK)
            top = None
            out = []
            for c in range(chunks):
                t = t_all[rows, c * 128 : (c + 1) * 128]
                top = t if top is None else jnp.maximum(top, t)
                out.append(jnp.maximum(best[c], fold_rows(t, jnp.maximum)))
            here = pl.ds(pl.multiple_of(i * CHUNK, CHUNK), CHUNK)
            row_m[here, :] = jnp.broadcast_to(jnp.max(top, axis=1, keepdims=True), (CHUNK, 128))
            return tuple(out)

        best = lax.fori_loop(
            0, steps, maxima, tuple(jnp.full((8, 128), LOW, F32) for _ in range(chunks)), unroll=True
        )
        best = [jnp.max(b, axis=0, keepdims=True) for b in best]

        def sums(i, total):
            rows = pl.ds(pl.multiple_of(slot * n + i * CHUNK, CHUNK), CHUNK)
            here = pl.ds(pl.multiple_of(i * CHUNK, CHUNK), CHUNK)
            m = row_m[here, :]
            p = pcol[rows, :]
            w = wcol[rows, :]
            out = []
            line = None
            for c in range(chunks):
                t = t_all[rows, c * 128 : (c + 1) * 128]
                d = t - m
                e = jnp.exp2(d)
                cd = t - best[c]
                ce = jnp.exp2(cd)
                at = p == ids[c]
                hit = jnp.where(at, t, 0.0)
                new = (e, e * d, hit)
                line = new if line is None else tuple(a + b for a, b in zip(line, new))
                for q, v in enumerate((ce, ce * cd, hit, jnp.where(at, w, 0.0))):
                    out.append(total[4 * c + q] + fold_rows(v, jnp.add))
            for q in range(3):
                lines[q, here, :] = line[q]
            return tuple(out)

        total = lax.fori_loop(
            0, steps, sums, tuple(jnp.zeros((8, 128), F32) for _ in range(4 * chunks)), unroll=True
        )
        total = [jnp.sum(b, axis=0, keepdims=True) for b in total]
        row = [row_m[...].T[0:1, :]] + [jnp.sum(lines[q].T, axis=0, keepdims=True) for q in range(3)]
        for q in range(4):
            for h in range(per):
                at = (q * nx + slot) * per + h
                rowst[0, at : at + 1, :] = row[q][:, h * 128 : (h + 1) * 128]
        return best, total

    parts = {}
    spread(0)
    i_core.wait_recv()
    scores(0, 0, 2)
    wp_r.wait_recv()
    wp_relay = start(remote(wp.at[1], wp.at[2], WP_RELAY, right))
    spread(1)
    wp_l.wait_recv()
    spread(3)

    i_pass = []

    def pass_on(q):
        i_y[q].wait_recv()
        i_pass.append(start(remote(i_rows(2, q), i_rows(3, q), I_PASS + q, at_yc(1))))

    pass_on(0)
    u_r0.wait_recv()
    relay_r = start(remote(u_rows(1, 0), u_rows(2, 0), U_RELAY_RIGHT, right))
    u_l1.wait_recv()
    relay_l = start(remote(u_rows(3, 1), u_rows(2, 1), U_RELAY_LEFT, left))
    pass_on(1)
    wp_relay.wait_recv()
    spread(2)
    pass_on(2)
    pass_on(3)
    scores(0, 2, 3)
    u_r1.wait_recv()
    scores(1, 0, 3)
    u_l0.wait_recv()
    scores(3, 0, 3)
    for c in i_pass:
        c.wait_recv()
    for slot in (0, 1, 3):
        scores(slot, 3, 4)
        parts[slot] = statistics(slot)
    def of_slot(s, c):
        return (parts[s][0][c],) + tuple(parts[s][1][4 * c : 4 * c + 4])

    def join(one, two):
        m = jnp.maximum(one[0], two[0])
        l = e = 0.0
        for v in (one, two):
            scale = jnp.exp2(v[0] - m)
            l = l + scale * v[1]
            e = e + scale * (v[2] + (v[0] - m) * v[1])
        return m, l, e, one[3] + two[3], one[4] + two[4]

    early = [join(join(of_slot(0, c), of_slot(1, c)), of_slot(3, c)) for c in range(chunks)]
    relay_r.wait_recv()
    relay_l.wait_recv()
    scores(2, 0, 4)
    parts[2] = statistics(2)

    rs_copies = [start(remote(rowst.at[0], rowst.at[d], RS_1 + d - 1, at_x(d))) for d in (2, 1, 3)]
    joined = [join(early[c], of_slot(2, c)) for c in range(chunks)]
    for c in range(chunks):
        b, h = c // per, c % per
        for q, v in enumerate(joined[c]):
            at = (q * nyc + b) * per + h
            colst[0, at : at + 1, :] = v
    cs_copies = [start(remote(colst.at[0], colst.at[d], CS_1 + d - 1, at_yc(d))) for d in (3, 2, 1)]

    @pl.when(z == 0)
    def _():
        @pl.when(high == 1)
        def _():
            greet(ready, next_y)

        pl.semaphore_wait(ready, 1)

        @pl.when(high == 0)
        def _():
            greet(ready, next_y)

        pl.semaphore_wait(hello, depth - 1)
        loop(1, depth, lambda to: greet(go, at_z(to)))

    def combine(ref, at, count, w):
        ms, ls, es, hits = (
            [ref[d, (q * count + at[d]) * per : (q * count + at[d] + 1) * per, :] for d in range(count)]
            for q in range(4)
        )
        m = functools.reduce(jnp.maximum, ms)
        scales = [jnp.exp2(mi - m) for mi in ms]
        l = sum(li * si for li, si in zip(ls, scales))
        e = sum(si * (ei + (mi - m) * li) for mi, li, ei, si in zip(ms, ls, es, scales))
        return m, l, w * (e / l - (sum(hits) - m))

    for c in cs_copies:
        c.wait_recv()
    columns = []
    for b in range(nyc):
        at = [b ^ d for d in range(nyc)]
        w = sum(colst[d, (4 * nyc + at[d]) * per : (4 * nyc + at[d] + 1) * per, :] for d in range(nyc))
        columns.append(combine(colst, at, nyc, w) + (w,))
    w_rows = [
        jnp.concatenate([wp[r, 0:1, h * 128 : (h + 1) * 128] for h in range(per)], axis=0) for r in range(nx)
    ]
    for c in rs_copies:
        c.wait_recv()
    rows_ = [combine(rowst, [(r - d) % nx for d in range(nx)], nx, w_rows[r]) + (w_rows[r],) for r in range(nx)]

    def line(v):
        v = jnp.sum(jnp.sum(v, axis=0, keepdims=True), axis=1, keepdims=True)
        return jnp.broadcast_to(v, (1, 128))

    first_half = lane < 64
    row_line = jnp.where(first_half, line(sum(v[2] for v in rows_)) * math.log(2.0), line(sum(w_rows)))
    column_line = jnp.where(first_half, line(sum(v[2] for v in columns)) * math.log(2.0), 0.0)
    mine[0] = row_line + column_line
    mine[1] = row_line
    mine[2] = column_line

    relations = 14

    def part_copy(r):
        return pltpu.make_async_remote_copy(
            src_ref=mine.at[0 if r < 2 else 1 if r < 8 else 2], dst_ref=parts_in.at[z * relations + r],
            send_sem=part_send.at[r], recv_sem=part_recv.at[0], device_id=at_plane(r), device_id_type=MESH,
        )

    own_part = pltpu.make_async_copy(mine.at[0], parts_in.at[0], part_recv.at[0])
    others = (11, 12, 13, 8, 9, 10, 5, 6, 7, 1, 2, 3, 4)

    @pl.when(z > 0)
    def _():
        pl.semaphore_wait(go, 1)
        part_copy(12).start()
        part_copy(0).start()

    @pl.when(z == 0)
    def _():
        own_part.start()
        part_copy(12).start()

    for r in others:
        if r != 12:
            part_copy(r).start()

    b_rows = []
    for m, l, _, w in columns:
        v = m + jnp.log2(l / w)
        b_rows += [v[h : h + 1, :] for h in range(per)]
    for r in (2, 1, 3, 0):
        m, l, _, w = rows_[r]
        a = m + jnp.log2(l / w)
        for h in range(per):
            acol[r * n + h * 128 : r * n + (h + 1) * 128, :] = jnp.broadcast_to(a[h : h + 1, :], (128, 128)).T

    def gradients(slot):
        def step(i, carry):
            rows = pl.ds(pl.multiple_of(slot * n + i * CHUNK, CHUNK), CHUNK)
            a = acol[rows, :]
            w2 = 2.0 * wcol[rows, :]
            p = pcol[rows, :]
            for c in range(chunks):
                t = t_all[rows, c * 128 : (c + 1) * 128]
                g = jnp.exp2(t - a) + jnp.exp2(t - b_rows[c])
                g = g - jnp.where(p == ids[c], w2, 0.0)
                g_all[rows, c * 128 : (c + 1) * 128] = g.astype(BF16)
            return carry

        lax.fori_loop(0, steps, step, 0, unroll=True)

    def user_part(slot):
        return jnp.dot(
            g_all[slot * n : (slot + 1) * n, :], i_all[...], preferred_element_type=F32
        )

    def item_part(slot):
        return dot_tn(g_all[:, slot * n : (slot + 1) * n], u_all[...])

    gradients(2)
    far[...] = user_part(2).astype(BF16)
    gu_fr = start(remote(far.at[pl.ds(0, half)], far_right, GU_FAR_RIGHT, right))
    gu_fl = start(remote(far.at[pl.ds(half, half)], far_left, GU_FAR_LEFT, left))
    gradients(1)
    own_gu[...] = user_part(1)
    to_left[0:half, :] = own_gu[0:half, :].astype(BF16)
    gu_l0 = start(remote(to_left.at[pl.ds(0, half)], from_right.at[pl.ds(0, half)], GU_LEFT_0, left))
    gradients(3)
    own_gi[...] = user_part(3)
    to_right[half:n, :] = own_gi[half:n, :].astype(BF16)
    gu_r1 = start(
        remote(to_right.at[pl.ds(half, half)], from_left.at[pl.ds(half, half)], GU_RIGHT_1, right)
    )
    gradients(0)
    core_1[...] = item_part(3).astype(BF16)
    gi_c1 = start(remote(core_1, got_core_1, GI_CORE_1, at_yc(1)))
    core_0[...] = item_part(1).astype(BF16)
    gi_c0 = start(remote(core_0, got_core_0, GI_CORE_0, at_yc(1)))
    other_gi[...] = item_part(2)
    gi_c1.wait_recv()
    to_y[...] = (other_gi[...] + got_core_1[...].astype(F32)).astype(BF16)
    gi_y = start(remote(to_y, from_y, GI_Y, at_yc(2)))

    gu_fr.wait_recv()
    to_right[0:half, :] = (own_gi[0:half, :] + far_right[...].astype(F32)).astype(BF16)
    gu_r0 = start(
        remote(to_right.at[pl.ds(0, half)], from_left.at[pl.ds(0, half)], GU_RIGHT_0, right)
    )
    gu_fl.wait_recv()
    to_left[half:n, :] = (own_gu[half:n, :] + far_left[...].astype(F32)).astype(BF16)
    gu_l1 = start(
        remote(to_left.at[pl.ds(half, half)], from_right.at[pl.ds(half, half)], GU_LEFT_1, left)
    )
    own_gu[...] = user_part(0)
    own_gi[...] = item_part(0)
    gi_c0.wait_recv()
    own_gi[...] = own_gi[...] + got_core_0[...].astype(F32)
    gu_l0.wait_recv()
    gu_r1.wait_recv()
    gu_r0.wait_recv()
    gu_l1.wait_recv()
    gu_out[...] = own_gu[...] + from_left[...].astype(F32) + from_right[...].astype(F32)
    gi_y.wait_recv()
    gi_out[...] = own_gi[...] + from_y[...].astype(F32)

    for c in started:
        c.wait_send()
    for r in others:
        part_copy(r).wait_send()

    @pl.when(z > 0)
    def _():
        part_copy(0).wait_send()

    def all_copy(to):
        return pltpu.make_async_remote_copy(
            src_ref=totals, dst_ref=totals, send_sem=all_send.at[to], recv_sem=all_recv.at[0],
            device_id=at_z(to), device_id_type=MESH,
        )

    @pl.when(z == 0)
    def _():
        pltpu.make_async_copy(parts_in, parts_in, part_recv.at[0]).wait()
        sums = [parts_in[i] for i in range(relations * depth)]
        while len(sums) > 1:
            sums = [sum(sums[i : i + 2]) for i in range(0, len(sums), 2)]
        totals[...] = sums[0]
        loop(1, depth, lambda to: all_copy(to).start())

    @pl.when(z > 0)
    def _():
        all_copy(0).wait_recv()

    sums = totals[...]
    weight = jnp.broadcast_to(sums[:, 64:65], (1, 128))
    scale_out[...] = jnp.broadcast_to(sums[:, 0:1] / weight, (8, 128))
    rows_total = float(n * n_blk * n_dp)
    factor = (rows_total / weight) * (k[:, 0:128] * math.log(2.0))
    factor_out[...] = jnp.concatenate([factor] * (width // 128), axis=1)

    @pl.when(z == 0)
    def _():
        loop(1, depth, lambda to: all_copy(to).wait_send())


def body(users, items, weights, positives, log_scale):
    users, items = users[0], items[0]
    n, width = users.shape
    n_blk, n_dp = lax.axis_size("blk"), lax.axis_size("dp")
    nyc = 4
    nx = n_blk // nyc
    any_space = pl.BlockSpec(memory_space=pl.ANY)
    vmem = pl.BlockSpec(memory_space=pltpu.VMEM)
    V = pltpu.VMEM
    rows, cols = nx * n, nyc * n
    half = n // 2
    gu, gi, scale, factor = pl.pallas_call(
        functools.partial(kernel, nx, nyc, n_dp, n_blk),
        out_shape=(
            V((n, width), F32),
            V((n, width), F32),
            V((8, 128), F32),
            V((1, width), F32),
        ),
        in_specs=[any_space] * 5,
        out_specs=(vmem,) * 4,
        scratch_shapes=[
            V((rows, width), BF16),
            V((cols, width), BF16),
            V((1, n), F32),
            V((1, n), jnp.int32),
            V((nx, 8, n), F32),
            V((rows, cols), F32),
            V((rows, cols), BF16),
            V((rows, 128), F32),
            V((rows, 128), F32),
            V((rows, 128), F32),
            V((n, 128), F32),
            V((3, n, 128), F32),
            V((nx, 4 * nx * n // 128, 128), F32),
            V((nyc, 5 * nyc * n // 128, 128), F32),
            pltpu.SMEM((1,), F32),
            V((n, width), BF16),
            V((half, width), BF16),
            V((half, width), BF16),
            V((n, width), BF16),
            V((n, width), BF16),
            V((n, width), BF16),
            V((n, width), BF16),
            V((n, width), F32),
            V((n, width), F32),
            V((n, width), F32),
            V((n, width), BF16),
            V((n, width), BF16),
            V((n, width), BF16),
            V((n, width), BF16),
            V((n, width), BF16),
            V((n, width), BF16),
            V((3, 1, 128), F32),
            V((14 * n_dp // 2, 1, 128), F32),
            V((1, 128), F32),
            pltpu.SemaphoreType.DMA((5,)),
            pltpu.SemaphoreType.DMA((TRANSFERS,)),
            pltpu.SemaphoreType.DMA((TRANSFERS,)),
            pltpu.SemaphoreType.DMA((14,)),
            pltpu.SemaphoreType.DMA((1,)),
            pltpu.SemaphoreType.DMA((n_dp // 2,)),
            pltpu.SemaphoreType.DMA((1,)),
            pltpu.SemaphoreType.REGULAR,
            pltpu.SemaphoreType.REGULAR,
            pltpu.SemaphoreType.REGULAR,
        ],
        compiler_params=pltpu.CompilerParams(
            collective_id=0, has_side_effects=True, vmem_limit_bytes=60 * 1024 * 1024
        ),
        cost_estimate=pl.CostEstimate(
            flops=6 * rows * cols * width, bytes_accessed=4 * n * width * 2,
            transcendentals=4 * rows * cols,
        ),
        name="loss_gradients",
    )(users, items, weights, positives, log_scale)
    return (gu * factor).astype(BF16)[None], (gi * factor).astype(BF16)[None], scale[0, 0:1]


def solution(mesh):
    placed = (P("dp", "blk", None), P("dp", "blk", None), P("dp", "blk"), P("dp", "blk"), P())
    return jax.shard_map(
        body,
        mesh=mesh,
        in_specs=placed,
        out_specs=(P("dp", "blk", None), P("dp", "blk", None), P()),
        check_vma=False,
    )
```

```python
import functools
import math

import jax
import jax.numpy as jnp
from jax import lax
from jax.experimental import pallas as pl
from jax.experimental.pallas import tpu as pltpu
from jax.sharding import PartitionSpec as P

MESH = pl.DeviceIdType.MESH
F32 = jnp.float32
BF16 = jnp.bfloat16
LOW = -3.0e38
CHUNK = 32

(
    U_RIGHT_0, U_LEFT_1, U_RIGHT_1, U_LEFT_0, U_RELAY_RIGHT, U_RELAY_LEFT,
    I_CORE, I_Y, I_Y_1, I_Y_2, I_Y_3, I_PASS, I_PASS_1, I_PASS_2, I_PASS_3,
    WP_RIGHT, WP_LEFT, WP_RELAY, RS_1, RS_2, RS_3, CS_1, CS_2, CS_3,
    GU_FAR_RIGHT, GU_FAR_LEFT, GU_RIGHT_0, GU_RIGHT_1, GU_LEFT_0, GU_LEFT_1,
    GI_CORE_0, GI_CORE_1, GI_Y, RX_0, RX_1, RX_2, RX_3, WX,
    TRANSFERS,
) = range(39)


def dot_nt(a, b):
    return lax.dot_general(a, b, (((1,), (1,)), ((), ())), preferred_element_type=F32)


def dot_tn(a, b):
    return lax.dot_general(a, b, (((0,), (0,)), ((), ())), preferred_element_type=F32)


def fold_rows(block, op):
    total = block[0:8]
    for r in range(8, block.shape[0], 8):
        total = op(total, block[r : r + 8])
    return total


def kernel(
    nx, nyc, n_dp, n_blk,
    users, items, weights, positives, log_scale,
    gu_out, gi_out, scale_out, factor_out,
    u_all, i_all, w_in, p_in, wp, t_all, g_all, wcol, pcol, acol, row_m, lines,
    rowst, other_rowst, other_w, colst, cpart, fold, w_rows, a_rows, b_tile, log_in,
    far, far_right, far_left, to_left, to_right, from_left, from_right,
    own_gu, own_gi, other_gi, core_0, core_1, got_core_0, got_core_1, to_y, from_y,
    mine, parts_in, totals,
    local_sem, send, recv, part_send, part_recv, all_send, all_recv, hello, ready, go,
):
    n = users.shape[0]
    width = users.shape[1]
    half = n // 2
    cols = nyc * n
    chunks = cols // 128
    per = n // 128
    steps = n // CHUNK
    me = lax.axis_index("blk")
    my_dp = lax.axis_index("dp")
    x = me // nyc
    yc = me % nyc
    core = yc % 2
    y = yc // 2
    depth = n_dp // 2
    z = my_dp % depth
    high = my_dp // depth

    def at_x(d):
        return {"blk": ((x + d) % nx) * nyc + yc, "dp": my_dp}

    def at_yc(d):
        c = 1 - core if d % 2 else core
        w = 1 - y if d // 2 else y
        return {"blk": x * nyc + w * 2 + c, "dp": my_dp}

    def at_z(to, c=1):
        return {"blk": x * nyc + y * 2 + c, "dp": high * depth + to}

    def at_plane(r):
        flip, dx = (r, 0) if r < 4 else ((r - 4) // 3, (r - 4) % 3 + 1)
        w = 1 - y if flip in (1, 2) else y
        v = 1 - high if flip in (1, 3) else high
        return {"blk": ((x + dx) % nx) * nyc + w * 2 + 1, "dp": v * depth}

    next_y = at_plane(1)

    right, left = at_x(1), at_x(nx - 1)

    def remote(src, dst, number, device):
        return pltpu.make_async_remote_copy(
            src_ref=src, dst_ref=dst, send_sem=send.at[number], recv_sem=recv.at[number],
            device_id=device, device_id_type=MESH,
        )

    def loop(first, last, action):
        def step(d, carry):
            action(d)
            return carry

        lax.fori_loop(first, last, step, 0)

    def greet(semaphore, device):
        pl.semaphore_signal(semaphore, inc=1, device_id=device, device_id_type=MESH)

    barrier = pltpu.get_barrier_semaphore()
    for device in (right, left, at_yc(1), at_yc(2)):
        greet(barrier, device)
    locals_ = [
        pltpu.make_async_copy(src, dst, local_sem.at[i])
        for i, (src, dst) in enumerate(
            [
                (weights, w_in),
                (positives, p_in),
                (users, u_all.at[pl.ds(0, n)]),
                (items, i_all.at[pl.ds(0, n)]),
                (log_scale, log_in),
            ]
        )
    ]
    for c in locals_:
        c.start()

    @pl.when((z == 0) & (core == 1))
    def _():
        loop(1, depth, lambda to: greet(barrier, at_z(to)))

        @pl.when(high == 0)
        def _():
            greet(barrier, next_y)

    wp[0] = jnp.zeros((8, n), F32)
    pl.semaphore_wait(barrier, 4 + jnp.where((core == 0) | (my_dp == 0), 0, 1))

    def u_rows(slot, h):
        return u_all.at[pl.ds(slot * n + h * half, half)]

    quarter = n // 4

    def i_rows(slot, q):
        return i_all.at[pl.ds(slot * n + q * quarter, quarter)]

    started = []

    def start(copy):
        copy.start()
        started.append(copy)
        return copy

    def piece(ref, h):
        return ref.at[pl.ds(h * half, half)]

    u_r0 = start(remote(piece(users, 0), u_rows(1, 0), U_RIGHT_0, right))
    u_l1 = start(remote(piece(users, 1), u_rows(3, 1), U_LEFT_1, left))
    i_y = [
        start(remote(items.at[pl.ds(q * quarter, quarter)], i_rows(2, q), I_Y + q, at_yc(2)))
        for q in range(4)
    ]
    i_core = start(remote(items, i_all.at[pl.ds(n, n)], I_CORE, at_yc(1)))
    locals_[0].wait()
    locals_[1].wait()
    wp[0, 0:1, :] = w_in[...]
    wp[0, 1:2, :] = p_in[...].astype(F32)
    wp_r = start(remote(wp.at[0], wp.at[1], WP_RIGHT, right))
    wp_l = start(remote(wp.at[0], wp.at[3], WP_LEFT, left))
    u_r1 = start(remote(piece(users, 1), u_rows(1, 1), U_RIGHT_1, right))
    u_l0 = start(remote(piece(users, 0), u_rows(3, 0), U_LEFT_0, left))
    for c in locals_[2:]:
        c.wait()

    @pl.when((z > 0) & (core == 1))
    def _():
        greet(hello, at_z(0))

    k = jnp.exp(jnp.full((1, 2 * n), log_in[0], F32)) * (1.0 / (math.sqrt(width) * math.log(2.0)))

    def scores(slot, first, last):
        block = dot_nt(u_all[slot * n : (slot + 1) * n, :], i_all[first * n : last * n, :])
        for b in range(last - first):
            t_all[slot * n : (slot + 1) * n, (first + b) * n : (first + b + 1) * n] = (
                block[:, b * n : (b + 1) * n] * k[:, 0:n]
            )

    lane = lax.broadcasted_iota(jnp.int32, (1, 128), 1)

    def column_ids(c):
        block, part = c // per, c % per
        owner = at_yc(block)["blk"]
        return (owner * n + part * 128 + lane).astype(F32)

    ids = [column_ids(c) for c in range(chunks)]

    def row_place(slot, h):
        return ((x + nx - slot) % nx) * per + h

    def column_place(c):
        return (at_yc(c // per)["blk"] % nyc) * per + c % per

    def spread(slot):
        for h in range(per):
            w_rows[pl.ds(row_place(slot, h), 1), :] = wp[slot, 0:1, h * 128 : (h + 1) * 128]
        wcol[slot * n : (slot + 1) * n, :] = jnp.broadcast_to(wp[slot, 0:1, :], (128, n)).T
        pcol[slot * n : (slot + 1) * n, :] = jnp.broadcast_to(wp[slot, 1:2, :], (128, n)).T

    def statistics(slot, rows_done=lambda: None):
        def maxima(i, best):
            rows = pl.ds(pl.multiple_of(slot * n + i * CHUNK, CHUNK), CHUNK)
            top = None
            out = []
            for c in range(chunks):
                t = t_all[rows, c * 128 : (c + 1) * 128]
                top = t if top is None else jnp.maximum(top, t)
                out.append(jnp.maximum(best[c], fold_rows(t, jnp.maximum)))
            here = pl.ds(pl.multiple_of(i * CHUNK, CHUNK), CHUNK)
            row_m[here, :] = jnp.broadcast_to(jnp.max(top, axis=1, keepdims=True), (CHUNK, 128))
            return tuple(out)

        best = lax.fori_loop(
            0, steps, maxima, tuple(jnp.full((8, 128), LOW, F32) for _ in range(chunks)), unroll=True
        )
        best = [jnp.max(b, axis=0, keepdims=True) for b in best]

        def sums(i, total):
            rows = pl.ds(pl.multiple_of(slot * n + i * CHUNK, CHUNK), CHUNK)
            here = pl.ds(pl.multiple_of(i * CHUNK, CHUNK), CHUNK)
            m = row_m[here, :]
            p = pcol[rows, :]
            w = wcol[rows, :]
            out = []
            line = None
            for c in range(chunks):
                t = t_all[rows, c * 128 : (c + 1) * 128]
                d = t - m
                e = jnp.exp2(d)
                cd = t - best[c]
                ce = jnp.exp2(cd)
                at = p == ids[c]
                hit = jnp.where(at, t, 0.0)
                new = (e, e * d, hit)
                line = new if line is None else tuple(a + b for a, b in zip(line, new))
                for q, v in enumerate((ce, ce * cd, hit, jnp.where(at, w, 0.0))):
                    out.append(total[4 * c + q] + fold_rows(v, jnp.add))
            for q in range(3):
                lines[q, here, :] = line[q]
            return tuple(out)

        total = lax.fori_loop(
            0, steps, sums, tuple(jnp.zeros((8, 128), F32) for _ in range(4 * chunks)), unroll=True
        )
        row = [row_m[...].T[0:1, :]] + [jnp.sum(lines[q].T, axis=0, keepdims=True) for q in range(3)]
        for q in range(4):
            for h in range(per):
                rowst[0, pl.ds(q * nx * per + row_place(slot, h), 1), :] = row[q][:, h * 128 : (h + 1) * 128]
        rows_done()
        for c in range(chunks):
            cpart[slot, pl.ds(column_place(c), 1), :] = best[c]
            for q in range(4):
                fold[q, pl.ds(pl.multiple_of(column_place(c) * 8, 8), 8), :] = total[4 * c + q]
        for q in range(4):
            cpart[slot, (q + 1) * chunks : (q + 2) * chunks, :] = sum(
                fold[q, pl.ds(r, chunks, stride=8), :] for r in range(8)
            )

    spread(0)
    i_core.wait_recv()
    scores(0, 0, 2)
    wp_r.wait_recv()
    wp_relay = start(remote(wp.at[1], wp.at[2], WP_RELAY, right))
    spread(1)
    wp_l.wait_recv()
    spread(3)

    i_pass = []

    def pass_on(q):
        i_y[q].wait_recv()
        i_pass.append(start(remote(i_rows(2, q), i_rows(3, q), I_PASS + q, at_yc(1))))

    pass_on(0)
    u_r0.wait_recv()
    relay_r = start(remote(u_rows(1, 0), u_rows(2, 0), U_RELAY_RIGHT, right))
    u_l1.wait_recv()
    relay_l = start(remote(u_rows(3, 1), u_rows(2, 1), U_RELAY_LEFT, left))
    pass_on(1)
    wp_relay.wait_recv()
    spread(2)
    weights_copy = remote(w_rows, other_w, WX, at_yc(1))

    @pl.when(core == 0)
    def _():
        weights_copy.start()

    pass_on(2)
    pass_on(3)
    scores(0, 2, 3)
    u_r1.wait_recv()
    scores(1, 0, 3)
    u_l0.wait_recv()
    scores(3, 0, 3)
    for c in i_pass:
        c.wait_recv()
    for slot in (0, 1, 3):
        scores(slot, 3, 4)
        statistics(slot)
    def of_slot(s):
        return [cpart[s, q * chunks : (q + 1) * chunks, :] for q in range(5)]

    def join(one, two):
        m = jnp.maximum(one[0], two[0])
        l = e = 0.0
        for v in (one, two):
            scale = jnp.exp2(v[0] - m)
            l = l + scale * v[1]
            e = e + scale * (v[2] + (v[0] - m) * v[1])
        return m, l, e, one[3] + two[3], one[4] + two[4]

    early = join(join(of_slot(0), of_slot(1)), of_slot(3))
    relay_r.wait_recv()
    relay_l.wait_recv()
    scores(2, 0, 4)
    def to_core_1(d):
        return remote(
            rowst.at[0], other_rowst.at[d], RX_0 + d, {"blk": ((x + d) % nx) * nyc + y * 2 + 1, "dp": my_dp}
        )

    def send_rows():
        @pl.when(core == 0)
        def _():
            for d in (2, 1, 3, 0):
                to_core_1(d).start()
            for d in (2, 1, 3):
                row_copy(d, 2).start()

        @pl.when(core == 1)
        def _():
            for d in (2, 1, 3):
                row_copy(d, 4).start()

    def row_copy(d, count):
        size = count * nx * per
        return remote(rowst.at[0, pl.ds(0, size)], rowst.at[d, pl.ds(0, size)], RS_1 + d - 1, at_x(d))

    def column_copy(d, count):
        size = count * chunks
        return remote(colst.at[0, pl.ds(0, size)], colst.at[d, pl.ds(0, size)], CS_1 + d - 1, at_yc(d))

    def column_counts(c):
        return ((3, 5), (1, 5), (2, 3)) if c == 0 else ((2, 5), (3, 3), (1, 3))

    statistics(2, send_rows)

    joined = join(early, of_slot(2))
    for q, v in enumerate((joined[0], joined[1], joined[4], joined[2], joined[3])):
        colst[0, q * chunks : (q + 1) * chunks, :] = v

    @pl.when(core == 0)
    def _():
        for d, count in column_counts(0):
            column_copy(d, count).start()

    @pl.when(core == 1)
    def _():
        for d, count in column_counts(1):
            column_copy(d, count).start()

    @pl.when((z == 0) & (core == 1))
    def _():
        @pl.when(high == 1)
        def _():
            greet(ready, next_y)

        pl.semaphore_wait(ready, 1)

        @pl.when(high == 0)
        def _():
            greet(ready, next_y)

        pl.semaphore_wait(hello, depth - 1)
        loop(1, depth, lambda to: greet(go, at_z(to)))

    def tiles(ref, count, q):
        size = count * per
        return [ref[d, q * size : (q + 1) * size, :] for d in range(count)]

    def combine(ref, count):
        ms, ls = tiles(ref, count, 0), tiles(ref, count, 1)
        m = functools.reduce(jnp.maximum, ms)
        scales = [jnp.exp2(mi - m) for mi in ms]
        return m, sum(li * si for li, si in zip(ls, scales)), scales

    def share(ref, count, w, es, hits, stats):
        m, l, scales = stats
        ms, ls = tiles(ref, count, 0), tiles(ref, count, 1)
        e = sum(si * (ei + (mi - m) * li) for mi, li, ei, si in zip(ms, ls, es, scales))
        return w * (e / l - (sum(hits) - m))

    @pl.when(core == 0)
    def _():
        for d in (1, 2, 3):
            column_copy(d, 3).wait_recv()
            row_copy(d, 2).wait_recv()

    @pl.when(core == 1)
    def _():
        for d in (1, 2, 3):
            column_copy(d, 5).wait_recv()
            row_copy(d, 4).wait_recv()

    def line(v):
        v = jnp.sum(jnp.sum(v, axis=0, keepdims=True), axis=1, keepdims=True)
        return jnp.broadcast_to(v, (1, 128))

    relations = 10

    def part_copy(r):
        return pltpu.make_async_remote_copy(
            src_ref=mine.at[0 if r < 2 else 1 if r < 4 else 2], dst_ref=parts_in.at[z * relations + r],
            send_sem=part_send.at[r], recv_sem=part_recv.at[0], device_id=at_plane(r), device_id_type=MESH,
        )

    others = (8, 7, 9, 5, 4, 6, 3, 1, 2)

    @pl.when(core == 1)
    def _():
        weights_copy.wait_recv()
        for d in range(nx):
            to_core_1(d).wait_recv()
        row_share = share(rowst, nx, w_rows[...], tiles(rowst, nx, 2), tiles(rowst, nx, 3), combine(rowst, nx))
        other_share = share(
            other_rowst, nx, other_w[...], tiles(other_rowst, nx, 2), tiles(other_rowst, nx, 3),
            combine(other_rowst, nx),
        )
        column_share = share(
            colst, nyc, sum(tiles(colst, nyc, 2)), tiles(colst, nyc, 3), tiles(colst, nyc, 4),
            combine(colst, nyc),
        )
        first_half = lane < 64
        row_line = jnp.where(
            first_half, line(row_share + other_share) * math.log(2.0), line(w_rows[...] + other_w[...])
        )
        column_line = jnp.where(first_half, line(column_share) * math.log(2.0), 0.0)
        mine[0] = row_line + column_line
        mine[1] = row_line
        mine[2] = column_line

        @pl.when(z > 0)
        def _():
            pl.semaphore_wait(go, 1)
            part_copy(0).start()

        @pl.when(z == 0)
        def _():
            pltpu.make_async_copy(mine.at[0], parts_in.at[0], part_recv.at[0]).start()

        for r in others:
            part_copy(r).start()

    m, l, _ = combine(colst, nyc)
    b_tile[...] = m + jnp.log2(l / sum(tiles(colst, nyc, 2)))
    m, l, _ = combine(rowst, nx)
    a_rows[...] = m + jnp.log2(l / w_rows[...])
    b_rows = [b_tile[pl.ds(column_place(c), 1), :] for c in range(chunks)]
    for r in (2, 1, 3, 0):
        for h in range(per):
            a = a_rows[pl.ds(row_place(r, h), 1), :]
            acol[r * n + h * 128 : r * n + (h + 1) * 128, :] = jnp.broadcast_to(a, (128, 128)).T

    def gradients(slot):
        def step(i, carry):
            rows = pl.ds(pl.multiple_of(slot * n + i * CHUNK, CHUNK), CHUNK)
            a = acol[rows, :]
            w2 = 2.0 * wcol[rows, :]
            p = pcol[rows, :]
            for c in range(chunks):
                t = t_all[rows, c * 128 : (c + 1) * 128]
                g = jnp.exp2(t - a) + jnp.exp2(t - b_rows[c])
                g = g - jnp.where(p == ids[c], w2, 0.0)
                g_all[rows, c * 128 : (c + 1) * 128] = g.astype(BF16)
            return carry

        lax.fori_loop(0, steps, step, 0, unroll=True)

    def user_part(slot):
        return jnp.dot(
            g_all[slot * n : (slot + 1) * n, :], i_all[...], preferred_element_type=F32
        )

    def item_part(slot):
        return dot_tn(g_all[:, slot * n : (slot + 1) * n], u_all[...])

    gradients(2)
    far[...] = user_part(2).astype(BF16)
    gu_fr = start(remote(far.at[pl.ds(0, half)], far_right, GU_FAR_RIGHT, right))
    gu_fl = start(remote(far.at[pl.ds(half, half)], far_left, GU_FAR_LEFT, left))
    gradients(1)
    own_gu[...] = user_part(1)
    to_left[0:half, :] = own_gu[0:half, :].astype(BF16)
    gu_l0 = start(remote(to_left.at[pl.ds(0, half)], from_right.at[pl.ds(0, half)], GU_LEFT_0, left))
    gradients(3)
    own_gi[...] = user_part(3)
    to_right[half:n, :] = own_gi[half:n, :].astype(BF16)
    gu_r1 = start(
        remote(to_right.at[pl.ds(half, half)], from_left.at[pl.ds(half, half)], GU_RIGHT_1, right)
    )
    gradients(0)
    core_1[...] = item_part(3).astype(BF16)
    gi_c1 = start(remote(core_1, got_core_1, GI_CORE_1, at_yc(1)))
    core_0[...] = item_part(1).astype(BF16)
    gi_c0 = start(remote(core_0, got_core_0, GI_CORE_0, at_yc(1)))
    other_gi[...] = item_part(2)
    gi_c1.wait_recv()
    to_y[...] = (other_gi[...] + got_core_1[...].astype(F32)).astype(BF16)
    gi_y = start(remote(to_y, from_y, GI_Y, at_yc(2)))

    gu_fr.wait_recv()
    to_right[0:half, :] = (own_gi[0:half, :] + far_right[...].astype(F32)).astype(BF16)
    gu_r0 = start(
        remote(to_right.at[pl.ds(0, half)], from_left.at[pl.ds(0, half)], GU_RIGHT_0, right)
    )
    gu_fl.wait_recv()
    to_left[half:n, :] = (own_gu[half:n, :] + far_left[...].astype(F32)).astype(BF16)
    gu_l1 = start(
        remote(to_left.at[pl.ds(half, half)], from_right.at[pl.ds(half, half)], GU_LEFT_1, left)
    )
    own_gu[...] = user_part(0)
    own_gi[...] = item_part(0)
    gi_c0.wait_recv()
    own_gi[...] = own_gi[...] + got_core_0[...].astype(F32)
    def all_copy(to, c):
        return pltpu.make_async_remote_copy(
            src_ref=totals, dst_ref=totals, send_sem=all_send.at[2 * to + c], recv_sem=all_recv.at[0],
            device_id=at_z(to, c), device_id_type=MESH,
        )

    gu_l0.wait_recv()
    gu_r1.wait_recv()
    gu_r0.wait_recv()
    gu_l1.wait_recv()
    gu_out[...] = own_gu[...] + from_left[...].astype(F32) + from_right[...].astype(F32)
    gi_y.wait_recv()
    gi_out[...] = own_gi[...] + from_y[...].astype(F32)

    for c in started:
        c.wait_send()
    @pl.when(core == 0)
    def _():
        weights_copy.wait_send()
        for d in range(nx):
            to_core_1(d).wait_send()
        for d in (1, 2, 3):
            row_copy(d, 2).wait_send()
        for d, count in column_counts(0):
            column_copy(d, count).wait_send()

    @pl.when(core == 1)
    def _():
        for d in (1, 2, 3):
            row_copy(d, 4).wait_send()
        for d, count in column_counts(1):
            column_copy(d, count).wait_send()
        for r in others:
            part_copy(r).wait_send()

        @pl.when(z > 0)
        def _():
            part_copy(0).wait_send()

    @pl.when((z == 0) & (core == 1))
    def _():
        pltpu.make_async_copy(parts_in, parts_in, part_recv.at[0]).wait()
        sums = [parts_in[i] for i in range(relations * depth)]
        while len(sums) > 1:
            sums = [sum(sums[i : i + 2]) for i in range(0, len(sums), 2)]
        totals[...] = sums[0]

        for to in range(1, min(5, depth)):
            all_copy(to, 0).start()
            all_copy(to, 1).start()
        all_copy(0, 0).start()
        loop(5, depth, lambda to: all_copy(to, 1).start())

    @pl.when((z > 0) | (core == 0))
    def _():
        all_copy(0, 0).wait_recv()

    pass_on_totals = (z > 4) & (core == 1)

    @pl.when(pass_on_totals)
    def _():
        all_copy(z, 0).start()

    sums = totals[...]
    weight = jnp.broadcast_to(sums[:, 64:65], (1, 128))
    scale_out[...] = jnp.broadcast_to(sums[:, 0:1] / weight, (8, 128))
    rows_total = float(n * n_blk * n_dp)
    factor = (rows_total / weight) * (k[:, 0:128] * math.log(2.0))
    factor_out[...] = jnp.concatenate([factor] * (width // 128), axis=1)

    @pl.when((z == 0) & (core == 1))
    def _():
        all_copy(0, 0).wait_send()
        loop(1, min(5, depth), lambda to: all_copy(to, 0).wait_send())
        loop(1, depth, lambda to: all_copy(to, 1).wait_send())

    @pl.when(pass_on_totals)
    def _():
        all_copy(z, 0).wait_send()


def body(users, items, weights, positives, log_scale):
    users, items = users[0], items[0]
    n, width = users.shape
    n_blk, n_dp = lax.axis_size("blk"), lax.axis_size("dp")
    nyc = 4
    nx = n_blk // nyc
    any_space = pl.BlockSpec(memory_space=pl.ANY)
    vmem = pl.BlockSpec(memory_space=pltpu.VMEM)
    V = pltpu.VMEM
    rows, cols = nx * n, nyc * n
    half = n // 2
    gu, gi, scale, factor = pl.pallas_call(
        functools.partial(kernel, nx, nyc, n_dp, n_blk),
        out_shape=(
            V((n, width), F32),
            V((n, width), F32),
            V((8, 128), F32),
            V((1, width), F32),
        ),
        in_specs=[any_space] * 5,
        out_specs=(vmem,) * 4,
        scratch_shapes=[
            V((rows, width), BF16),
            V((cols, width), BF16),
            V((1, n), F32),
            V((1, n), jnp.int32),
            V((nx, 8, n), F32),
            V((rows, cols), F32),
            V((rows, cols), BF16),
            V((rows, 128), F32),
            V((rows, 128), F32),
            V((rows, 128), F32),
            V((n, 128), F32),
            V((3, n, 128), F32),
            V((nx, 4 * nx * n // 128, 128), F32),
            V((nx, 4 * nx * n // 128, 128), F32),
            V((rows // 128, 128), F32),
            V((nyc, 5 * cols // 128, 128), F32),
            V((nx, 5 * cols // 128, 128), F32),
            V((4, 8 * cols // 128, 128), F32),
            V((rows // 128, 128), F32),
            V((rows // 128, 128), F32),
            V((cols // 128, 128), F32),
            pltpu.SMEM((1,), F32),
            V((n, width), BF16),
            V((half, width), BF16),
            V((half, width), BF16),
            V((n, width), BF16),
            V((n, width), BF16),
            V((n, width), BF16),
            V((n, width), BF16),
            V((n, width), F32),
            V((n, width), F32),
            V((n, width), F32),
            V((n, width), BF16),
            V((n, width), BF16),
            V((n, width), BF16),
            V((n, width), BF16),
            V((n, width), BF16),
            V((n, width), BF16),
            V((3, 1, 128), F32),
            V((10 * n_dp // 2, 1, 128), F32),
            V((1, 128), F32),
            pltpu.SemaphoreType.DMA((5,)),
            pltpu.SemaphoreType.DMA((TRANSFERS,)),
            pltpu.SemaphoreType.DMA((TRANSFERS,)),
            pltpu.SemaphoreType.DMA((10,)),
            pltpu.SemaphoreType.DMA((1,)),
            pltpu.SemaphoreType.DMA((n_dp,)),
            pltpu.SemaphoreType.DMA((1,)),
            pltpu.SemaphoreType.REGULAR,
            pltpu.SemaphoreType.REGULAR,
            pltpu.SemaphoreType.REGULAR,
        ],
        compiler_params=pltpu.CompilerParams(
            collective_id=0, has_side_effects=True, vmem_limit_bytes=60 * 1024 * 1024
        ),
        cost_estimate=pl.CostEstimate(
            flops=6 * rows * cols * width, bytes_accessed=4 * n * width * 2,
            transcendentals=4 * rows * cols,
        ),
        name="loss_gradients",
    )(users, items, weights, positives, log_scale)
    return (gu * factor).astype(BF16)[None], (gi * factor).astype(BF16)[None], scale[0, 0:1]


def solution(mesh):
    placed = (P("dp", "blk", None), P("dp", "blk", None), P("dp", "blk"), P("dp", "blk"), P())
    return jax.shard_map(
        body,
        mesh=mesh,
        in_specs=placed,
        out_specs=(P("dp", "blk", None), P("dp", "blk", None), P()),
        check_vma=False,
    )
```

```python
import functools
import math

import jax
import jax.numpy as jnp
from jax import lax
from jax.experimental import pallas as pl
from jax.experimental.pallas import tpu as pltpu
from jax.sharding import PartitionSpec as P

MESH = pl.DeviceIdType.MESH
F32 = jnp.float32
BF16 = jnp.bfloat16
LOW = -3.0e38
CHUNK = 64

(
    U_RIGHT_0, U_LEFT_1, U_RIGHT_1, U_LEFT_0, U_RELAY_RIGHT, U_RELAY_LEFT,
    I_CORE, I_Y, I_Y_1, I_Y_2, I_Y_3, I_PASS, I_PASS_1, I_PASS_2, I_PASS_3,
    WP_RIGHT, WP_LEFT, WP_RELAY, RS_1, RS_2, RS_3, CS_1, CS_2, CS_3,
    GU_FAR_RIGHT, GU_FAR_LEFT, GU_RIGHT_0, GU_RIGHT_1, GU_LEFT_0, GU_LEFT_1,
    GI_CORE_0, GI_CORE_1, GI_Y, RX_0, RX_1, RX_2, RX_3, WX,
    TRANSFERS,
) = range(39)


def dot_nt(a, b):
    return lax.dot_general(a, b, (((1,), (1,)), ((), ())), preferred_element_type=F32)


def dot_tn(a, b):
    return lax.dot_general(a, b, (((0,), (0,)), ((), ())), preferred_element_type=F32)


def fold_rows(block, op):
    total = block[0:8]
    for r in range(8, block.shape[0], 8):
        total = op(total, block[r : r + 8])
    return total


def kernel(
    nx, nyc, n_dp, n_blk,
    users, items, weights, positives, log_scale,
    gu_out, gi_out, scale_out, factor_out,
    u_all, i_all, w_in, p_in, wp, t_all, g_all, wcol, pcol, acol, row_m, lines,
    rowst, other_rowst, other_w, colst, cpart, fold, w_rows, a_rows, b_tile, log_in,
    far, far_right, far_left, to_left, to_right, from_left, from_right,
    own_gu, own_gi, other_gi, core_0, core_1, got_core_0, got_core_1, to_y, from_y,
    mine, parts_in, totals,
    local_sem, send, recv, part_send, part_recv, all_send, all_recv, hello, ready, go,
):
    n = users.shape[0]
    width = users.shape[1]
    half = n // 2
    cols = nyc * n
    chunks = cols // 128
    per = n // 128
    steps = n // CHUNK
    me = lax.axis_index("blk")
    my_dp = lax.axis_index("dp")
    x = me // nyc
    yc = me % nyc
    core = yc % 2
    y = yc // 2
    depth = n_dp // 2
    z = my_dp % depth
    high = my_dp // depth

    def at_x(d):
        return {"blk": ((x + d) % nx) * nyc + yc, "dp": my_dp}

    def at_yc(d):
        c = 1 - core if d % 2 else core
        w = 1 - y if d // 2 else y
        return {"blk": x * nyc + w * 2 + c, "dp": my_dp}

    def at_z(to, c=1):
        return {"blk": x * nyc + y * 2 + c, "dp": high * depth + to}

    def at_plane(r):
        flip, dx = (r, 0) if r < 4 else ((r - 4) // 3, (r - 4) % 3 + 1)
        w = 1 - y if flip in (1, 2) else y
        v = 1 - high if flip in (1, 3) else high
        return {"blk": ((x + dx) % nx) * nyc + w * 2 + 1, "dp": v * depth}

    next_y = at_plane(1)

    right, left = at_x(1), at_x(nx - 1)

    def remote(src, dst, number, device):
        return pltpu.make_async_remote_copy(
            src_ref=src, dst_ref=dst, send_sem=send.at[number], recv_sem=recv.at[number],
            device_id=device, device_id_type=MESH,
        )

    def loop(first, last, action):
        def step(d, carry):
            action(d)
            return carry

        lax.fori_loop(first, last, step, 0)

    def greet(semaphore, device):
        pl.semaphore_signal(semaphore, inc=1, device_id=device, device_id_type=MESH)

    barrier = pltpu.get_barrier_semaphore()
    for device in (right, left, at_yc(1), at_yc(2)):
        greet(barrier, device)
    locals_ = [
        pltpu.make_async_copy(src, dst, local_sem.at[i])
        for i, (src, dst) in enumerate(
            [
                (weights, w_in),
                (positives, p_in),
                (users, u_all.at[pl.ds(0, n)]),
                (items, i_all.at[pl.ds(0, n)]),
                (log_scale, log_in),
            ]
        )
    ]
    for c in locals_:
        c.start()

    @pl.when((z == 0) & (core == 1))
    def _():
        loop(1, depth, lambda to: greet(barrier, at_z(to)))

        @pl.when(high == 0)
        def _():
            greet(barrier, next_y)

    wp[0] = jnp.zeros((8, n), F32)
    pl.semaphore_wait(barrier, 4 + jnp.where((core == 0) | (my_dp == 0), 0, 1))

    def u_rows(slot, h):
        return u_all.at[pl.ds(slot * n + h * half, half)]

    quarter = n // 4

    def i_rows(slot, q):
        return i_all.at[pl.ds(slot * n + q * quarter, quarter)]

    started = []

    def start(copy):
        copy.start()
        started.append(copy)
        return copy

    def piece(ref, h):
        return ref.at[pl.ds(h * half, half)]

    u_r0 = start(remote(piece(users, 0), u_rows(1, 0), U_RIGHT_0, right))
    u_l1 = start(remote(piece(users, 1), u_rows(3, 1), U_LEFT_1, left))
    i_y = [
        start(remote(items.at[pl.ds(q * quarter, quarter)], i_rows(2, q), I_Y + q, at_yc(2)))
        for q in range(4)
    ]
    i_core = start(remote(items, i_all.at[pl.ds(n, n)], I_CORE, at_yc(1)))
    locals_[0].wait()
    locals_[1].wait()
    wp[0, 0:1, :] = w_in[...]
    wp[0, 1:2, :] = p_in[...].astype(F32)
    wp_r = start(remote(wp.at[0], wp.at[1], WP_RIGHT, right))
    wp_l = start(remote(wp.at[0], wp.at[3], WP_LEFT, left))
    u_r1 = start(remote(piece(users, 1), u_rows(1, 1), U_RIGHT_1, right))
    u_l0 = start(remote(piece(users, 0), u_rows(3, 0), U_LEFT_0, left))
    for c in locals_[2:]:
        c.wait()

    @pl.when((z > 0) & (core == 1))
    def _():
        greet(hello, at_z(0))

    k = jnp.exp(jnp.full((1, 2 * n), log_in[0], F32)) * (1.0 / (math.sqrt(width) * math.log(2.0)))

    def scores(slot, first, last):
        block = dot_nt(u_all[slot * n : (slot + 1) * n, :], i_all[first * n : last * n, :])
        for b in range(last - first):
            t_all[slot * n : (slot + 1) * n, (first + b) * n : (first + b + 1) * n] = (
                block[:, b * n : (b + 1) * n] * k[:, 0:n]
            )

    lane = lax.broadcasted_iota(jnp.int32, (1, 128), 1)

    def column_ids(c):
        block, part = c // per, c % per
        owner = at_yc(block)["blk"]
        return (owner * n + part * 128 + lane).astype(F32)

    ids = [column_ids(c) for c in range(chunks)]

    def row_place(slot, h):
        return ((x + nx - slot) % nx) * per + h

    def column_place(c):
        return (at_yc(c // per)["blk"] % nyc) * per + c % per

    def spread(slot):
        for h in range(per):
            w_rows[pl.ds(row_place(slot, h), 1), :] = wp[slot, 0:1, h * 128 : (h + 1) * 128]
        wcol[slot * n : (slot + 1) * n, :] = jnp.broadcast_to(wp[slot, 0:1, :], (128, n)).T
        pcol[slot * n : (slot + 1) * n, :] = jnp.broadcast_to(wp[slot, 1:2, :], (128, n)).T

    def statistics(slot, rows_done=lambda: None):
        def maxima(i, best):
            rows = pl.ds(pl.multiple_of(slot * n + i * CHUNK, CHUNK), CHUNK)
            top = None
            out = []
            for c in range(chunks):
                t = t_all[rows, c * 128 : (c + 1) * 128]
                top = t if top is None else jnp.maximum(top, t)
                out.append(jnp.maximum(best[c], fold_rows(t, jnp.maximum)))
            here = pl.ds(pl.multiple_of(i * CHUNK, CHUNK), CHUNK)
            row_m[here, :] = jnp.broadcast_to(jnp.max(top, axis=1, keepdims=True), (CHUNK, 128))
            return tuple(out)

        best = lax.fori_loop(
            0, steps, maxima, tuple(jnp.full((8, 128), LOW, F32) for _ in range(chunks)), unroll=True
        )
        best = [jnp.max(b, axis=0, keepdims=True) for b in best]

        def sums(i, total):
            rows = pl.ds(pl.multiple_of(slot * n + i * CHUNK, CHUNK), CHUNK)
            here = pl.ds(pl.multiple_of(i * CHUNK, CHUNK), CHUNK)
            m = row_m[here, :]
            p = pcol[rows, :]
            w = wcol[rows, :]
            out = []
            line = None
            for c in range(chunks):
                t = t_all[rows, c * 128 : (c + 1) * 128]
                d = t - m
                e = jnp.exp2(d)
                cd = t - best[c]
                ce = jnp.exp2(cd)
                at = p == ids[c]
                hit = jnp.where(at, t, 0.0)
                new = (e, e * d, hit)
                line = new if line is None else tuple(a + b for a, b in zip(line, new))
                for q, v in enumerate((ce, ce * cd, hit, jnp.where(at, w, 0.0))):
                    out.append(total[4 * c + q] + fold_rows(v, jnp.add))
            for q in range(3):
                lines[q, here, :] = line[q]
            return tuple(out)

        total = lax.fori_loop(
            0, steps, sums, tuple(jnp.zeros((8, 128), F32) for _ in range(4 * chunks)), unroll=True
        )
        row = [row_m[...].T[0:1, :]] + [jnp.sum(lines[q].T, axis=0, keepdims=True) for q in range(3)]
        for q in range(4):
            for h in range(per):
                rowst[0, pl.ds(q * nx * per + row_place(slot, h), 1), :] = row[q][:, h * 128 : (h + 1) * 128]
        rows_done()
        for c in range(chunks):
            cpart[slot, pl.ds(column_place(c), 1), :] = best[c]
            for q in range(4):
                fold[q, pl.ds(pl.multiple_of(column_place(c) * 8, 8), 8), :] = total[4 * c + q]
        for q in range(4):
            cpart[slot, (q + 1) * chunks : (q + 2) * chunks, :] = sum(
                fold[q, pl.ds(r, chunks, stride=8), :] for r in range(8)
            )

    spread(0)
    i_core.wait_recv()
    scores(0, 0, 2)
    wp_r.wait_recv()
    wp_relay = start(remote(wp.at[1], wp.at[2], WP_RELAY, right))
    spread(1)
    wp_l.wait_recv()
    spread(3)

    i_pass = []

    def pass_on(q):
        i_y[q].wait_recv()
        i_pass.append(start(remote(i_rows(2, q), i_rows(3, q), I_PASS + q, at_yc(1))))

    pass_on(0)
    u_r0.wait_recv()
    relay_r = start(remote(u_rows(1, 0), u_rows(2, 0), U_RELAY_RIGHT, right))
    u_l1.wait_recv()
    relay_l = start(remote(u_rows(3, 1), u_rows(2, 1), U_RELAY_LEFT, left))
    pass_on(1)
    wp_relay.wait_recv()
    spread(2)
    weights_copy = remote(w_rows, other_w, WX, at_yc(1))

    @pl.when(core == 0)
    def _():
        weights_copy.start()

    pass_on(2)
    pass_on(3)
    scores(0, 2, 3)
    u_r1.wait_recv()
    scores(1, 0, 3)
    u_l0.wait_recv()
    scores(3, 0, 3)
    for c in i_pass:
        c.wait_recv()
    for slot in (0, 1, 3):
        scores(slot, 3, 4)
        statistics(slot)
    def of_slot(s):
        return [cpart[s, q * chunks : (q + 1) * chunks, :] for q in range(5)]

    def join(one, two):
        m = jnp.maximum(one[0], two[0])
        l = e = 0.0
        for v in (one, two):
            scale = jnp.exp2(v[0] - m)
            l = l + scale * v[1]
            e = e + scale * (v[2] + (v[0] - m) * v[1])
        return m, l, e, one[3] + two[3], one[4] + two[4]

    early = join(join(of_slot(0), of_slot(1)), of_slot(3))
    relay_r.wait_recv()
    relay_l.wait_recv()
    scores(2, 0, 4)
    def to_core_1(d):
        return remote(
            rowst.at[0], other_rowst.at[d], RX_0 + d, {"blk": ((x + d) % nx) * nyc + y * 2 + 1, "dp": my_dp}
        )

    def send_rows():
        @pl.when(core == 0)
        def _():
            for d in (2, 1, 3, 0):
                to_core_1(d).start()
            for d in (2, 1, 3):
                row_copy(d, 2).start()

        @pl.when(core == 1)
        def _():
            for d in (2, 1, 3):
                row_copy(d, 4).start()

    def row_copy(d, count):
        size = count * nx * per
        return remote(rowst.at[0, pl.ds(0, size)], rowst.at[d, pl.ds(0, size)], RS_1 + d - 1, at_x(d))

    def column_copy(d, count):
        size = count * chunks
        return remote(colst.at[0, pl.ds(0, size)], colst.at[d, pl.ds(0, size)], CS_1 + d - 1, at_yc(d))

    def column_counts(c):
        return ((3, 5), (1, 5), (2, 3)) if c == 0 else ((2, 5), (3, 3), (1, 3))

    statistics(2, send_rows)

    joined = join(early, of_slot(2))
    for q, v in enumerate((joined[0], joined[1], joined[4], joined[2], joined[3])):
        colst[0, q * chunks : (q + 1) * chunks, :] = v

    @pl.when(core == 0)
    def _():
        for d, count in column_counts(0):
            column_copy(d, count).start()

    @pl.when(core == 1)
    def _():
        for d, count in column_counts(1):
            column_copy(d, count).start()

    @pl.when((z == 0) & (core == 1))
    def _():
        @pl.when(high == 1)
        def _():
            greet(ready, next_y)

        pl.semaphore_wait(ready, 1)

        @pl.when(high == 0)
        def _():
            greet(ready, next_y)

        pl.semaphore_wait(hello, depth - 1)
        loop(1, depth, lambda to: greet(go, at_z(to)))

    def tiles(ref, count, q):
        size = count * per
        return [ref[d, q * size : (q + 1) * size, :] for d in range(count)]

    def combine(ref, count):
        ms, ls = tiles(ref, count, 0), tiles(ref, count, 1)
        m = functools.reduce(jnp.maximum, ms)
        scales = [jnp.exp2(mi - m) for mi in ms]
        return m, sum(li * si for li, si in zip(ls, scales)), scales

    def share(ref, count, w, es, hits, stats):
        m, l, scales = stats
        ms, ls = tiles(ref, count, 0), tiles(ref, count, 1)
        e = sum(si * (ei + (mi - m) * li) for mi, li, ei, si in zip(ms, ls, es, scales))
        return w * (e / l - (sum(hits) - m))

    @pl.when(core == 0)
    def _():
        for d in (1, 2, 3):
            column_copy(d, 3).wait_recv()
            row_copy(d, 2).wait_recv()

    @pl.when(core == 1)
    def _():
        for d in (1, 2, 3):
            column_copy(d, 5).wait_recv()
            row_copy(d, 4).wait_recv()

    def line(v):
        v = jnp.sum(jnp.sum(v, axis=0, keepdims=True), axis=1, keepdims=True)
        return jnp.broadcast_to(v, (1, 128))

    relations = 10

    def part_copy(r):
        return pltpu.make_async_remote_copy(
            src_ref=mine.at[0 if r < 2 else 1 if r < 4 else 2], dst_ref=parts_in.at[z * relations + r],
            send_sem=part_send.at[r], recv_sem=part_recv.at[0], device_id=at_plane(r), device_id_type=MESH,
        )

    others = (8, 7, 9, 5, 4, 6, 3, 1, 2)

    @pl.when(core == 1)
    def _():
        weights_copy.wait_recv()
        for d in range(nx):
            to_core_1(d).wait_recv()
        row_share = share(rowst, nx, w_rows[...], tiles(rowst, nx, 2), tiles(rowst, nx, 3), combine(rowst, nx))
        other_share = share(
            other_rowst, nx, other_w[...], tiles(other_rowst, nx, 2), tiles(other_rowst, nx, 3),
            combine(other_rowst, nx),
        )
        column_share = share(
            colst, nyc, sum(tiles(colst, nyc, 2)), tiles(colst, nyc, 3), tiles(colst, nyc, 4),
            combine(colst, nyc),
        )
        first_half = lane < 64
        row_line = jnp.where(
            first_half, line(row_share + other_share) * math.log(2.0), line(w_rows[...] + other_w[...])
        )
        column_line = jnp.where(first_half, line(column_share) * math.log(2.0), 0.0)
        mine[0] = row_line + column_line
        mine[1] = row_line
        mine[2] = column_line

        @pl.when(z > 0)
        def _():
            pl.semaphore_wait(go, 1)
            part_copy(0).start()

        @pl.when(z == 0)
        def _():
            pltpu.make_async_copy(mine.at[0], parts_in.at[0], part_recv.at[0]).start()

        for r in others:
            part_copy(r).start()

    m, l, _ = combine(colst, nyc)
    b_tile[...] = m + jnp.log2(l / sum(tiles(colst, nyc, 2)))
    m, l, _ = combine(rowst, nx)
    a_rows[...] = m + jnp.log2(l / w_rows[...])
    b_rows = [b_tile[pl.ds(column_place(c), 1), :] for c in range(chunks)]
    for r in (2, 1, 3, 0):
        for h in range(per):
            a = a_rows[pl.ds(row_place(r, h), 1), :]
            acol[r * n + h * 128 : r * n + (h + 1) * 128, :] = jnp.broadcast_to(a, (128, 128)).T

    def gradients(slot):
        def step(i, carry):
            rows = pl.ds(pl.multiple_of(slot * n + i * CHUNK, CHUNK), CHUNK)
            a = acol[rows, :]
            w2 = 2.0 * wcol[rows, :]
            p = pcol[rows, :]
            for c in range(chunks):
                t = t_all[rows, c * 128 : (c + 1) * 128]
                g = jnp.exp2(t - a) + jnp.exp2(t - b_rows[c])
                g = g - jnp.where(p == ids[c], w2, 0.0)
                g_all[rows, c * 128 : (c + 1) * 128] = g.astype(BF16)
            return carry

        lax.fori_loop(0, steps, step, 0, unroll=True)

    def user_part(slot):
        return jnp.dot(
            g_all[slot * n : (slot + 1) * n, :], i_all[...], preferred_element_type=F32
        )

    def item_part(slot):
        return dot_tn(g_all[:, slot * n : (slot + 1) * n], u_all[...])

    gradients(2)
    far[...] = user_part(2).astype(BF16)
    gu_fr = start(remote(far.at[pl.ds(0, half)], far_right, GU_FAR_RIGHT, right))
    gu_fl = start(remote(far.at[pl.ds(half, half)], far_left, GU_FAR_LEFT, left))
    gradients(1)
    own_gu[...] = user_part(1)
    to_left[0:half, :] = own_gu[0:half, :].astype(BF16)
    gu_l0 = start(remote(to_left.at[pl.ds(0, half)], from_right.at[pl.ds(0, half)], GU_LEFT_0, left))
    gradients(3)
    own_gi[...] = user_part(3)
    to_right[half:n, :] = own_gi[half:n, :].astype(BF16)
    gu_r1 = start(
        remote(to_right.at[pl.ds(half, half)], from_left.at[pl.ds(half, half)], GU_RIGHT_1, right)
    )
    gradients(0)
    core_1[...] = item_part(3).astype(BF16)
    gi_c1 = start(remote(core_1, got_core_1, GI_CORE_1, at_yc(1)))
    core_0[...] = item_part(1).astype(BF16)
    gi_c0 = start(remote(core_0, got_core_0, GI_CORE_0, at_yc(1)))
    other_gi[...] = item_part(2)
    gi_c1.wait_recv()
    to_y[...] = (other_gi[...] + got_core_1[...].astype(F32)).astype(BF16)
    gi_y = start(remote(to_y, from_y, GI_Y, at_yc(2)))

    gu_fr.wait_recv()
    to_right[0:half, :] = (own_gi[0:half, :] + far_right[...].astype(F32)).astype(BF16)
    gu_r0 = start(
        remote(to_right.at[pl.ds(0, half)], from_left.at[pl.ds(0, half)], GU_RIGHT_0, right)
    )
    gu_fl.wait_recv()
    to_left[half:n, :] = (own_gu[half:n, :] + far_left[...].astype(F32)).astype(BF16)
    gu_l1 = start(
        remote(to_left.at[pl.ds(half, half)], from_right.at[pl.ds(half, half)], GU_LEFT_1, left)
    )
    own_gu[...] = user_part(0)
    own_gi[...] = item_part(0)
    gi_c0.wait_recv()
    own_gi[...] = own_gi[...] + got_core_0[...].astype(F32)
    def all_copy(to, c):
        return pltpu.make_async_remote_copy(
            src_ref=totals, dst_ref=totals, send_sem=all_send.at[2 * to + c], recv_sem=all_recv.at[0],
            device_id=at_z(to, c), device_id_type=MESH,
        )

    gu_l0.wait_recv()
    gu_r1.wait_recv()
    gu_r0.wait_recv()
    gu_l1.wait_recv()
    gu_out[...] = own_gu[...] + from_left[...].astype(F32) + from_right[...].astype(F32)
    gi_y.wait_recv()
    gi_out[...] = own_gi[...] + from_y[...].astype(F32)

    for c in started:
        c.wait_send()
    @pl.when(core == 0)
    def _():
        weights_copy.wait_send()
        for d in range(nx):
            to_core_1(d).wait_send()
        for d in (1, 2, 3):
            row_copy(d, 2).wait_send()
        for d, count in column_counts(0):
            column_copy(d, count).wait_send()

    @pl.when(core == 1)
    def _():
        for d in (1, 2, 3):
            row_copy(d, 4).wait_send()
        for d, count in column_counts(1):
            column_copy(d, count).wait_send()
        for r in others:
            part_copy(r).wait_send()

        @pl.when(z > 0)
        def _():
            part_copy(0).wait_send()

    @pl.when((z == 0) & (core == 1))
    def _():
        pltpu.make_async_copy(parts_in, parts_in, part_recv.at[0]).wait()
        sums = [parts_in[i] for i in range(relations * depth)]
        while len(sums) > 1:
            sums = [sum(sums[i : i + 2]) for i in range(0, len(sums), 2)]
        totals[...] = sums[0]

        for to in range(1, min(5, depth)):
            all_copy(to, 0).start()
            all_copy(to, 1).start()
        all_copy(0, 0).start()
        loop(5, depth, lambda to: all_copy(to, 1).start())

    @pl.when((z > 0) | (core == 0))
    def _():
        all_copy(0, 0).wait_recv()

    pass_on_totals = (z > 4) & (core == 1)

    @pl.when(pass_on_totals)
    def _():
        all_copy(z, 0).start()

    sums = totals[...]
    weight = jnp.broadcast_to(sums[:, 64:65], (1, 128))
    scale_out[...] = jnp.broadcast_to(sums[:, 0:1] / weight, (8, 128))
    rows_total = float(n * n_blk * n_dp)
    factor = (rows_total / weight) * (k[:, 0:128] * math.log(2.0))
    factor_out[...] = jnp.concatenate([factor] * (width // 128), axis=1)

    @pl.when((z == 0) & (core == 1))
    def _():
        all_copy(0, 0).wait_send()
        loop(1, min(5, depth), lambda to: all_copy(to, 0).wait_send())
        loop(1, depth, lambda to: all_copy(to, 1).wait_send())

    @pl.when(pass_on_totals)
    def _():
        all_copy(z, 0).wait_send()


def body(users, items, weights, positives, log_scale):
    users, items = users[0], items[0]
    n, width = users.shape
    n_blk, n_dp = lax.axis_size("blk"), lax.axis_size("dp")
    nyc = 4
    nx = n_blk // nyc
    any_space = pl.BlockSpec(memory_space=pl.ANY)
    vmem = pl.BlockSpec(memory_space=pltpu.VMEM)
    V = pltpu.VMEM
    rows, cols = nx * n, nyc * n
    half = n // 2
    gu, gi, scale, factor = pl.pallas_call(
        functools.partial(kernel, nx, nyc, n_dp, n_blk),
        out_shape=(
            V((n, width), F32),
            V((n, width), F32),
            V((8, 128), F32),
            V((1, width), F32),
        ),
        in_specs=[any_space] * 5,
        out_specs=(vmem,) * 4,
        scratch_shapes=[
            V((rows, width), BF16),
            V((cols, width), BF16),
            V((1, n), F32),
            V((1, n), jnp.int32),
            V((nx, 8, n), F32),
            V((rows, cols), F32),
            V((rows, cols), BF16),
            V((rows, 128), F32),
            V((rows, 128), F32),
            V((rows, 128), F32),
            V((n, 128), F32),
            V((3, n, 128), F32),
            V((nx, 4 * nx * n // 128, 128), F32),
            V((nx, 4 * nx * n // 128, 128), F32),
            V((rows // 128, 128), F32),
            V((nyc, 5 * cols // 128, 128), F32),
            V((nx, 5 * cols // 128, 128), F32),
            V((4, 8 * cols // 128, 128), F32),
            V((rows // 128, 128), F32),
            V((rows // 128, 128), F32),
            V((cols // 128, 128), F32),
            pltpu.SMEM((1,), F32),
            V((n, width), BF16),
            V((half, width), BF16),
            V((half, width), BF16),
            V((n, width), BF16),
            V((n, width), BF16),
            V((n, width), BF16),
            V((n, width), BF16),
            V((n, width), F32),
            V((n, width), F32),
            V((n, width), F32),
            V((n, width), BF16),
            V((n, width), BF16),
            V((n, width), BF16),
            V((n, width), BF16),
            V((n, width), BF16),
            V((n, width), BF16),
            V((3, 1, 128), F32),
            V((10 * n_dp // 2, 1, 128), F32),
            V((1, 128), F32),
            pltpu.SemaphoreType.DMA((5,)),
            pltpu.SemaphoreType.DMA((TRANSFERS,)),
            pltpu.SemaphoreType.DMA((TRANSFERS,)),
            pltpu.SemaphoreType.DMA((10,)),
            pltpu.SemaphoreType.DMA((1,)),
            pltpu.SemaphoreType.DMA((n_dp,)),
            pltpu.SemaphoreType.DMA((1,)),
            pltpu.SemaphoreType.REGULAR,
            pltpu.SemaphoreType.REGULAR,
            pltpu.SemaphoreType.REGULAR,
        ],
        compiler_params=pltpu.CompilerParams(
            collective_id=0, has_side_effects=True, vmem_limit_bytes=60 * 1024 * 1024
        ),
        cost_estimate=pl.CostEstimate(
            flops=6 * rows * cols * width, bytes_accessed=4 * n * width * 2,
            transcendentals=4 * rows * cols,
        ),
        name="loss_gradients",
    )(users, items, weights, positives, log_scale)
    return (gu * factor).astype(BF16)[None], (gi * factor).astype(BF16)[None], scale[0, 0:1]


def solution(mesh):
    placed = (P("dp", "blk", None), P("dp", "blk", None), P("dp", "blk"), P("dp", "blk"), P())
    return jax.shard_map(
        body,
        mesh=mesh,
        in_specs=placed,
        out_specs=(P("dp", "blk", None), P("dp", "blk", None), P()),
        check_vma=False,
    )
```
